256 devices in a mesh: dom: 16 (over z, y_lo), near: 16 (over y_hi, x, core).
Axes of the slice: x: 4, y: 4 (y_hi: 2, y_lo: 2; y = y_hi * 2 + y_lo), z: 8, core: 2. Of those that a mesh axis runs over, the one named last changes fastest.
Arguments:
- solution: float32 [56, 9, 32768], P(None, None, ('dom', 'near')), may hold values from -6 to 6
- star_matrices: float32 [3, 9, 9, 32768], P(None, None, None, ('dom', 'near')), may hold values from -2.5 to 2.5
- flux_plus: float32 [4, 9, 9, 32768], P(None, None, None, ('dom', 'near')), may hold values from -1.2 to 1.2
- flux_minus: float32 [4, 9, 9, 32768], P(None, None, None, ('dom', 'near')), may hold values from -1.2 to 1.2
- stiffness: float32 [3, 56, 56], replicated, may hold values from -0.75 to 0.75
- face_lift: float32 [4, 56, 21], replicated, may hold values from -0.625 to 0.625
- face_project: float32 [4, 21, 56], replicated, may hold values from -0.75 to 0.75
- cluster: int32 [32768], P(('dom', 'near')), may hold values from 0 to 1, as said below
- neighbour_part: int32 [4, 32768], P(None, ('dom', 'near')), may hold values from 0 to 4, as said below
- neighbour_slot: int32 [4, 32768], P(None, ('dom', 'near')), may hold values from 0 to 127, as said below
- neighbour_face: int32 [4, 32768], P(None, ('dom', 'near')), may hold values from 0 to 3
- orientation: int32 [4, 32768], P(None, ('dom', 'near')), may hold values from 0 to 2
- halo_send: int32 [4, 4096], P(None, ('dom', 'near')), may hold values from 0 to 127, as said below
Outputs:
- updated: float32 [56, 9, 32768], P(None, None, ('dom', 'near'))
The draws below stay inside these ranges and needn't reach their ends.
Inputs may be any that keep to these rules, and one draw needn't show every extreme that they name: 0 marks an element that takes two half steps, 1 one that takes one step of length one. A partition holds at most 64 elements of cluster 0, and some partition exactly that many. `neighbour_part`: 0: the neighbour lies in the element's own partition; 1 to 4: it comes from the partition at near -1, near +1, dom -1, dom +1 (cyclic). In each partition each pair of a part p of 1 to 4 and a slot below 16 is named by exactly one face. `neighbour_slot`: an element of the own partition where the part is 0, a slot below 16 otherwise. `halo_send`: row r of a partition lists the elements it sends to the partition at near +1, near -1, dom +1, dom -1 for r = 0, 1, 2, 3; the 16 entries of a row are distinct.
All inputs are finite; a program needn't handle non-finite values.
Results may differ from the reference program's by a relative error of at most 0.0003.
Values sent between devices are 32-bit elements; how exact they have to be, the bound alone decides.
A program may use at most 128 MiB of HBM per device.

```python
import math
import jax
import jax.numpy as jnp
import numpy as np
from jax import lax

MODES = 56
FIELDS = 9
FACE_MODES = 21
ORDER = 6
E_DEV = 128
HALO = 16
SMALL_MAX = 64
NE = 32768
N_DOM = 16
N_NEAR = 16


def draw_cluster(key, part):
    partitions = NE // E_DEV
    count_key, top_key, order_key = jax.random.split(key, 3)
    counts = jax.random.randint(count_key, (partitions,), 1, SMALL_MAX + 1)
    busiest = jax.random.randint(top_key, (), 0, partitions)
    counts = jnp.where(jnp.arange(partitions) == busiest, SMALL_MAX, counts)
    orders = jax.vmap(lambda subkey: jax.random.permutation(subkey, E_DEV))(jax.random.split(order_key, partitions))
    return jnp.where(orders < counts[:, None], 0, 1).astype(jnp.int32).reshape(NE)


def neighbour_tables(key):
    partitions = NE // E_DEV
    face_count = 4 * E_DEV
    order_key, slot_key = jax.random.split(key)
    orders = jax.vmap(lambda subkey: jax.random.permutation(subkey, face_count))(jax.random.split(order_key, partitions))
    ranks = jax.vmap(lambda permuted: jnp.zeros(face_count, jnp.int32).at[permuted].set(jnp.arange(face_count, dtype=jnp.int32)))(orders)
    halo_faces = ranks < 4 * HALO
    local_slots = jax.random.randint(slot_key, (partitions, face_count), 0, E_DEV)
    parts = jnp.where(halo_faces, 1 + ranks // HALO, 0)
    slots = jnp.where(halo_faces, ranks % HALO, local_slots)
    parts = jnp.transpose(parts.reshape(partitions, 4, E_DEV), (1, 0, 2)).reshape(4, NE)
    slots = jnp.transpose(slots.reshape(partitions, 4, E_DEV), (1, 0, 2)).reshape(4, NE)
    return (parts.astype(jnp.int32), slots.astype(jnp.int32))


def draw_neighbour_part(key, part):
    return neighbour_tables(jax.random.fold_in(key, 11))[0]


def draw_neighbour_slot(key, part):
    return neighbour_tables(jax.random.fold_in(key, 11))[1]


def draw_halo_send(key, part):
    partitions = NE // E_DEV
    subkeys = jax.random.split(jax.random.fold_in(key, 23), partitions * 4)
    lists = jax.vmap(lambda subkey: jax.random.permutation(subkey, E_DEV)[:HALO])(subkeys).reshape(partitions, 4, HALO)
    return jnp.transpose(lists, (1, 0, 2)).reshape(4, partitions * HALO).astype(jnp.int32)


def with_ends(result, key, low, high):
    longest = result.shape.index(max(result.shape))
    spots = []
    for shift in (0, 1):
        where = [jax.random.randint(jax.random.fold_in(key, axis), (), 0, length) for axis, length in enumerate(result.shape)]
        where[longest] = (where[longest] + shift) % result.shape[longest]
        spots.append(tuple(where))
    return result.at[spots[0]].set(low).at[spots[1]].set(high)


def block_levels(own_key, shape, cuts, low, top_value):
    def one(position, shards_of):
        heights = jax.random.uniform(jax.random.fold_in(jax.random.fold_in(own_key, 6), position), (shards_of,), jnp.float32, low / len(cuts), top_value / len(cuts))
        return jnp.repeat(jnp.exp(heights), shape[position] // shards_of).reshape((-1,) + (1,) * (len(shape) - position - 1))

    gain = one(*cuts[0])
    for cut in cuts[1:]:
        gain = gain * one(*cut)
    return gain


def noise(key, extent, width, limit, pieces=(), kind=jnp.bfloat16):
    entries = jax.random.normal(key, extent, jnp.float32) * width
    if len(pieces) > 0:
        entries = block_levels(key, extent, pieces, -0.22, 0.18) * entries
    return jnp.clip(entries, min=-limit, max=limit).astype(kind)


def setup_inputs(seed: int = 0) -> dict:
    keys = jax.random.split(jax.random.key(seed), 14)
    solution = noise(keys[0], (MODES, FIELDS, NE), 1.0, 6.0, ((2, 256),), jnp.float32)
    star_matrices = noise(keys[1], (3, FIELDS, FIELDS, NE), 0.45, 2.5, ((3, 256),), jnp.float32)
    flux_plus = noise(keys[2], (4, FIELDS, FIELDS, NE), 0.2, 1.2, ((3, 256),), jnp.float32)
    flux_minus = noise(keys[3], (4, FIELDS, FIELDS, NE), 0.2, 1.2, ((3, 256),), jnp.float32)
    stiffness = noise(keys[4], (3, MODES, MODES), MODES ** -0.5, 0.75, (), jnp.float32)
    face_lift = noise(keys[5], (4, MODES, FACE_MODES), (4 * FACE_MODES) ** -0.5, 0.625, (), jnp.float32)
    face_project = noise(keys[6], (4, FACE_MODES, MODES), MODES ** -0.5, 0.75, (), jnp.float32)
    cluster = draw_cluster(jax.random.fold_in(keys[13], 71), 0)
    neighbour_part = draw_neighbour_part(jax.random.fold_in(keys[13], 71), 0)
    neighbour_slot = draw_neighbour_slot(jax.random.fold_in(keys[13], 71), 0)
    neighbour_face = with_ends(jax.random.randint(keys[10], (4, NE), 0, 4), jax.random.fold_in(keys[10], 1), 0, 3).astype(jnp.int32)
    orientation = with_ends(jax.random.randint(keys[11], (4, NE), 0, 3), jax.random.fold_in(keys[11], 1), 0, 2).astype(jnp.int32)
    halo_send = draw_halo_send(jax.random.fold_in(keys[13], 71), 0)
    return dict(solution=solution, star_matrices=star_matrices, flux_plus=flux_plus, flux_minus=flux_minus, stiffness=stiffness, face_lift=face_lift, face_project=face_project, cluster=cluster, neighbour_part=neighbour_part, neighbour_slot=neighbour_slot, neighbour_face=neighbour_face, orientation=orientation, halo_send=halo_send)


precise = lax.Precision.HIGHEST


def rotations():
    degree = ORDER - 1
    node_list = [(a, b) for a in range(degree + 1) for b in range(degree + 1 - a)]
    lookup = {point_ab: number for number, point_ab in enumerate(node_list)}
    tables = []
    for rotation in range(3):
        table_row = []
        for point_ab in node_list:
            triple = (point_ab[0], point_ab[1], degree - point_ab[0] - point_ab[1])
            rolled = triple[rotation:] + triple[:rotation]
            table_row.append(lookup[(rolled[0], rolled[1])])
        tables.append(table_row)
    return np.array(tables, dtype=np.int32)


def integral_weights(begin_time, end_time):
    return [(end_time ** (exponent + 1) - begin_time ** (exponent + 1)) / math.factorial(exponent + 1) for exponent in range(ORDER)]


def star_apply(field, star_matrices):
    return jnp.einsum("mfe,dfge->dmge", field, star_matrices, precision=precise)


def taylor_stack(initial, star_matrices, stiffness):
    elements = initial.shape[2]
    forward = jnp.transpose(stiffness, (1, 0, 2)).reshape(MODES, 3 * MODES)
    layers = [initial]
    for exponent in range(ORDER - 1):
        starred = star_apply(layers[-1], star_matrices).reshape(3 * MODES, FIELDS * elements)
        layers.append(jnp.dot(forward, starred, precision=precise).reshape(MODES, FIELDS, elements))
    return layers


def time_integral(layers, begin_time, end_time):
    weights = integral_weights(begin_time, end_time)
    summed = weights[0] * layers[0]
    for exponent in range(1, ORDER):
        summed = summed + weights[exponent] * layers[exponent]
    return summed


def volume_term(integral, star_matrices, stiffness):
    elements = integral.shape[2]
    backward = jnp.transpose(stiffness, (2, 0, 1)).reshape(MODES, 3 * MODES)
    starred = star_apply(integral, star_matrices).reshape(3 * MODES, FIELDS * elements)
    return jnp.dot(backward, starred, precision=precise).reshape(MODES, FIELDS, elements)


def element_update(base_state, integral, gathered, star_matrices, stiffness, flux_plus, flux_minus, face_lift, face_project):
    elements = integral.shape[2]
    projected = jnp.dot(face_project.reshape(4 * FACE_MODES, MODES), integral.reshape(MODES, FIELDS * elements), precision=precise).reshape(4, FACE_MODES, FIELDS, elements)
    inside = jnp.einsum("ipfe,ifge->ipge", projected, flux_plus, precision=precise)
    outside = jnp.einsum("ipfe,ifge->ipge", gathered, flux_minus, precision=precise)
    lifting = jnp.transpose(face_lift, (1, 0, 2)).reshape(MODES, 4 * FACE_MODES)
    lifted = jnp.dot(lifting, (inside + outside).reshape(4 * FACE_MODES, FIELDS * elements), precision=precise).reshape(MODES, FIELDS, elements)
    return base_state + volume_term(integral, star_matrices, stiffness) - lifted


def reference(solution, star_matrices, flux_plus, flux_minus, stiffness, face_lift, face_project, cluster, neighbour_part, neighbour_slot, neighbour_face, orientation, halo_send):
    blocks = NE // E_DEV
    block_ids = jnp.arange(blocks, dtype=jnp.int32)
    combined = face_project[:, rotations(), :].reshape(12, FACE_MODES, MODES)

    def cut(array, block):
        return lax.dynamic_slice_in_dim(array, block * E_DEV, E_DEV, array.ndim - 1)

    def spread(stacked):
        return jnp.transpose(stacked, (1, 2, 0, 3)).reshape(MODES, FIELDS, NE)

    def global_sources(block):
        parts = cut(neighbour_part, block)
        slots = cut(neighbour_slot, block)
        row_pos = block // N_NEAR
        col_pos = block % N_NEAR
        senders = jnp.stack([row_pos * N_NEAR + (col_pos - 1) % N_NEAR, row_pos * N_NEAR + (col_pos + 1) % N_NEAR, ((row_pos - 1) % N_DOM) * N_NEAR + col_pos, ((row_pos + 1) % N_DOM) * N_NEAR + col_pos]).astype(jnp.int32)
        direction = jnp.clip(parts - 1, 0, 3)
        sender = senders[direction]
        sent = halo_send[direction, sender * HALO + jnp.minimum(slots, HALO - 1)]
        return jnp.where(parts == 0, block * E_DEV + slots, sender * E_DEV + sent).astype(jnp.int32)

    def gathered_faces(buffer, block):
        source_ids = global_sources(block)
        source_data = jnp.take(buffer, source_ids, axis=2)
        choose = cut(neighbour_face, block) * 3 + cut(orientation, block)
        selected = jnp.take(combined, choose, axis=0)
        return jnp.einsum("iepm,mfie->ipfe", selected, source_data, precision=precise)

    def matrices(block):
        return (cut(star_matrices, block), stiffness, cut(flux_plus, block), cut(flux_minus, block), face_lift, face_project)

    def section_one(block):
        layers = taylor_stack(cut(solution, block), cut(star_matrices, block), stiffness)
        return (time_integral(layers, 0.0, 0.5), time_integral(layers, 0.5, 1.0), time_integral(layers, 0.0, 1.0))

    first_half, second_half, whole_step = [spread(stacked) for stacked in lax.map(section_one, block_ids)]

    def section_two(block):
        base_state = cut(solution, block)
        is_small = (cut(cluster, block) == 0)[None, None, :]
        moved = element_update(base_state, cut(first_half, block), gathered_faces(first_half, block), *matrices(block))
        middle = jnp.where(is_small, moved, base_state)
        layers = taylor_stack(middle, cut(star_matrices, block), stiffness)
        later = jnp.where(is_small, time_integral(layers, 0.0, 0.5), cut(second_half, block))
        return (middle, later)

    middle_state, later_half = [spread(stacked) for stacked in lax.map(section_two, block_ids)]
    summed = first_half + later_half

    def section_three(block):
        is_small = (cut(cluster, block) == 0)[None, None, :]
        small_new = element_update(cut(middle_state, block), cut(later_half, block), gathered_faces(later_half, block), *matrices(block))
        large_new = element_update(cut(solution, block), cut(whole_step, block), gathered_faces(summed, block), *matrices(block))
        return jnp.where(is_small, small_new, large_new)

    return spread(lax.map(section_three, block_ids))
```

```python
import functools
import math

import jax
import jax.numpy as jnp
from jax import lax
from jax.experimental import pallas as pl
from jax.experimental.pallas import tpu as pltpu
from jax.sharding import PartitionSpec as P

MESH = pl.DeviceIdType.MESH
MODES = 56
FIELDS = 9
FACE_MODES = 21
ORDER = 6
E = 128
HALO = 16
KPAD = 64
FACE_PAD = 24
FACES = 4 * FACE_PAD
COLS = FIELDS * E
GROUPS = ((0, 1), (2, 3), (4, 5), (6, 7), (8,))
BF = jnp.bfloat16
F32 = jnp.float32


def orbit_nodes():
    degree = ORDER - 1
    nodes = [(a, b, degree - a - b) for a in range(degree + 1) for b in range(degree + 1 - a)]
    number = {node: n for n, node in enumerate(nodes)}
    seen, orbits = set(), []
    for node in nodes:
        if node in seen:
            continue
        a, b, c = node
        orbit = [(a, b, c), (b, c, a), (c, a, b)]
        seen.update(orbit)
        orbits.append([number[member] for member in orbit])
    order = [-1] * FACE_PAD
    for o, orbit in enumerate(orbits):
        for c in range(3):
            order[c * 8 + o] = orbit[c]
    return order


ORDERED = orbit_nodes()


def weights(begin, end):
    return [
        (end ** (k + 1) - begin ** (k + 1)) / math.factorial(k + 1) for k in range(ORDER)
    ]


def dot(a, b):
    return jnp.dot(a, b, preferred_element_type=F32)


def iota(shape, dim):
    return lax.broadcasted_iota(jnp.int32, shape, dim)


def ones_where(condition):
    return jnp.where(condition, 1.0, 0.0).astype(F32)


def high_low(x):
    high = x.astype(BF).astype(F32)
    return high, x - high


def place(x, marks):
    high, rest = high_low(x)
    middle, low = high_low(rest)
    marks = marks.astype(BF)
    return dot(high.astype(BF), marks) + dot(middle.astype(BF), marks) + dot(low.astype(BF), marks)


def place_left(marks, x):
    high, rest = high_low(x)
    middle, low = high_low(rest)
    marks = marks.astype(BF)
    return dot(marks, high.astype(BF)) + dot(marks, middle.astype(BF)) + dot(marks, low.astype(BF))


def threefold(matrix):
    high, low = high_low(matrix)
    row, col = iota((MODES, 3 * KPAD), 0), iota((MODES, 3 * KPAD), 1)
    twice = ones_where((col == row) | (col == row + KPAD)).astype(BF)
    last = ones_where(col == row + 2 * KPAD).astype(BF)
    return (dot(high.astype(BF), twice) + dot(low.astype(BF), last)).astype(BF)


def kernel(
    n_dom,
    n_near,
    sol_ref,
    star_ref,
    plus_ref,
    minus_ref,
    stiff_ref,
    lift_ref,
    proj_ref,
    cluster_ref,
    part_ref,
    slot_ref,
    nface_ref,
    turn_ref,
    halo_ref,
    out_ref,
    r_ref,
    y_ref,
    first_ref,
    second_ref,
    base_ref,
    x_ref,
    g_ref,
    prev_ref,
    a_ref,
    b_ref,
    p_ref,
    l_ref,
    ohl_ref,
    ohr_ref,
    ohs_ref,
    send_buf,
    recv_buf,
    send_sem,
    recv_sem,
):
    dom, near = lax.axis_index("dom"), lax.axis_index("near")
    targets = (
        (dom, lax.rem(near + 1, n_near)),
        (dom, lax.rem(near + n_near - 1, n_near)),
        (lax.rem(dom + 1, n_dom), near),
        (lax.rem(dom + n_dom - 1, n_dom), near),
    )
    barrier = pltpu.get_barrier_semaphore()
    for target in targets:
        pl.semaphore_signal(barrier, inc=1, device_id=target, device_id_type=MESH)

    def cols(f, count=1):
        return slice(f * E, (f + count) * E)

    stiff = jnp.concatenate([stiff_ref[d] for d in range(3)], axis=0)
    a_ref[...] = threefold(stiff)

    def split_into(t, f):
        high, low = high_low(t)
        zero = jnp.zeros((KPAD - MODES, E), F32)
        high = jnp.concatenate([high, zero], axis=0).astype(BF)
        low = jnp.concatenate([low, zero], axis=0).astype(BF)
        r_ref[0:KPAD, cols(f)] = high
        r_ref[KPAD : 2 * KPAD, cols(f)] = low
        r_ref[2 * KPAD : 3 * KPAD, cols(f)] = high

    def multiply(matrix, rows, group, slot):
        span = cols(group[0], len(group))
        y_ref[slot, 0:rows, span] = dot(matrix[...], r_ref[:, span])

    def star(group, slot, row0=0):
        totals = [None] * len(group)
        for d in range(3):
            for f in range(FIELDS):
                y = y_ref[slot, row0 + d * MODES : row0 + (d + 1) * MODES, cols(f)]
                for n, g in enumerate(group):
                    term = star_ref[f, g, d : d + 1, :] * y
                    totals[n] = term if totals[n] is None else totals[n] + term
        return totals

    half, rest = weights(0.0, 0.5), weights(0.5, 1.0)

    def pick(table, k):
        value = jnp.float32(table[0])
        for n in range(1, len(table)):
            value = jnp.where(k == n, jnp.float32(table[n]), value)
        return value

    small = cluster_ref[...] == 0

    for group in GROUPS:
        for f in group:
            u = sol_ref[f]
            split_into(u, f)
            first_ref[f] = half[0] * u
            second_ref[f] = rest[0] * u
        multiply(a_ref, 3 * MODES, group, 0)

    backward = jnp.concatenate([stiff_ref[d].T for d in range(3)], axis=0)
    node, entry = iota((FACE_PAD, FACE_MODES), 1), iota((FACE_PAD, FACE_MODES), 0)
    chosen = entry < 0
    for spot, number in enumerate(ORDERED):
        if number >= 0:
            chosen = chosen | ((entry == spot) & (node == number))
    chosen = ones_where(chosen)
    project = jnp.concatenate([place_left(chosen, proj_ref[:, j, :]) for j in range(4)], axis=0)
    lifts = jnp.concatenate([place_left(chosen, lift_ref[:, j, :]) for j in range(4)], axis=0)
    b_ref[...] = threefold(jnp.concatenate([project, backward], axis=0))
    p_ref[...] = threefold(project)
    lift_high, lift_low = high_low(lifts.T)
    row, col = iota((FACES, 2 * FACES), 0), iota((FACES, 2 * FACES), 1)
    twice = ones_where((col == row) | (col == row + FACES)).astype(BF)
    once = ones_where(col == row).astype(BF)
    l_ref[...] = jnp.concatenate(
        [dot(lift_high.astype(BF), twice), dot(lift_low.astype(BF), once)], axis=0
    ).astype(BF)

    part, slot_of = part_ref[...], slot_ref[...]
    face_of = nface_ref[...]
    local_key = jnp.where(part == 0, face_of * E + slot_of, -1)
    remote_key = jnp.where(part > 0, face_of * (4 * HALO) + (part - 1) * HALO + slot_of, -1)
    for i in range(4):
        ohl_ref[:, cols(i)] = ones_where(local_key[i : i + 1, :] == iota((4 * E, E), 0)).astype(BF)
        ohr_ref[:, cols(i)] = ones_where(
            remote_key[i : i + 1, :] == iota((16 * HALO, E), 0)
        ).astype(BF)
    spread = ones_where(iota((HALO, E), 0) == lax.rem(iota((HALO, E), 1), HALO)).astype(BF)
    sent = dot(halo_ref[...].astype(F32).astype(BF), spread)
    for r in range(4):
        ohs_ref[:, cols(r)] = ones_where(
            sent[r : r + 1, :] == iota((2 * E, E), 0).astype(F32)
        ).astype(BF) + ones_where(
            sent[r : r + 1, :] + float(E) == iota((2 * E, E), 0).astype(F32)
        ).astype(BF)

    lane = iota((1, E), 1)
    lane_group = lane // HALO

    def taylor_rest(first_only):
        def body(k, carry):
            old, new = lax.rem(k, 2), lax.rem(k + 1, 2)
            w1, w2 = pick(half, k + 1), pick(rest, k + 1)
            for group in GROUPS:
                for g, t in zip(group, star(group, old)):
                    split_into(t, g)
                    first_ref[g] += w1 * t
                    if not first_only:
                        second_ref[g] += w2 * t
                multiply(a_ref, 3 * MODES, group, new)
            return carry

        lax.fori_loop(0, ORDER - 2, body, 0)
        for group in GROUPS:
            for g, t in zip(group, star(group, 0)):
                value = first_ref[g] + half[5] * t
                if first_only:
                    value = jnp.where(small, value, second_ref[g])
                else:
                    second_ref[g] += rest[5] * t
                first_ref[g] = value

    def exchange(phase):
        copies = []
        highs, lows = [], []
        for f in range(FIELDS):
            high, low = high_low(first_ref[f])
            highs.append(high)
            lows.append(low)
        stacked = jnp.concatenate(
            [
                jnp.concatenate(highs, axis=0).astype(BF),
                jnp.concatenate(lows, axis=0).astype(BF),
            ],
            axis=1,
        )
        taken = dot(stacked, ohs_ref[...])
        for r in range(4):
            block = taken[:, cols(r)]
            packed = block[0:MODES]
            for f in range(1, 8):
                packed = jnp.where(lane_group == f, block[f * MODES : (f + 1) * MODES], packed)
            tail = block[8 * MODES : 8 * MODES + 8]
            for k in range(1, 7):
                start = 8 * MODES + 8 * k
                tail = jnp.where(lane_group == k, block[start : start + 8], tail)
            send_buf[phase, r] = jnp.concatenate([packed, tail], axis=0)
        if phase == 0:
            pl.semaphore_wait(barrier, 4)
        for r in range(4):
            copy = pltpu.make_async_remote_copy(
                src_ref=send_buf.at[phase, r],
                dst_ref=recv_buf.at[phase, r],
                send_sem=send_sem.at[phase, r],
                recv_sem=recv_sem.at[phase, r],
                device_id=targets[r],
                device_id_type=MESH,
            )
            copy.start()
            copies.append(copy)
        return copies

    def gather(blocks, marks):
        sides = []
        for block in blocks:
            high, low = high_low(block)
            sides.append(jnp.concatenate([high, low], axis=0).astype(BF))
        both = dot(jnp.concatenate(sides, axis=1), marks[...])
        rows = FIELDS * FACE_PAD
        return both[0:rows] + both[rows : 2 * rows]

    def by_field(read):
        return jnp.concatenate([read(f) for f in range(FIELDS)], axis=0)

    def local_part():
        for group in GROUPS:
            for f in group:
                split_into(first_ref[f], f)
            multiply(b_ref, FACES + 3 * MODES, group, 0)
        g_ref[...] = gather(
            [
                by_field(lambda f: y_ref[0, j * FACE_PAD : (j + 1) * FACE_PAD, cols(f)])
                for j in range(4)
            ],
            ohl_ref,
        )
        for i in range(4):
            totals = [None] * FIELDS
            for f in range(FIELDS):
                y = y_ref[0, i * FACE_PAD : (i + 1) * FACE_PAD, cols(f)]
                for g in range(FIELDS):
                    term = plus_ref[f, g, i : i + 1, :] * y
                    totals[g] = term if totals[g] is None else totals[g] + term
            for g in range(FIELDS):
                x_ref[i * FACE_PAD : (i + 1) * FACE_PAD, cols(g)] = totals[g]
        for group in GROUPS:
            for g, v in zip(group, star(group, 0, FACES)):
                base_ref[g] += v

    def remote_part(phase, copies):
        for copy in copies:
            copy.wait()
        rolled = []
        for r in range(4):
            block = recv_buf[phase, r]
            rolled.append(
                [block if c == 0 else pltpu.roll(block, c * HALO, 1) for c in range(8)]
            )

        def collect(at, rows):
            value = None
            for spot in range(8):
                r = spot % 4
                piece = rolled[r][(spot - at) % 8][rows]
                value = piece if value is None else jnp.where(lane_group == spot, piece, value)
            return value

        for group in GROUPS:
            for f in group:
                if f < 8:
                    split_into(collect(f, slice(0, MODES)), f)
                else:
                    tiles = [collect(k, slice(MODES, MODES + 8)) for k in range(7)]
                    split_into(jnp.concatenate(tiles, axis=0), f)
            multiply(p_ref, FACES, group, 1)

        def pair(j):
            def read(f):
                low = y_ref[1, j * FACE_PAD : (j + 1) * FACE_PAD, cols(f)]
                high = y_ref[1, (j + 1) * FACE_PAD : (j + 2) * FACE_PAD, cols(f)]
                return jnp.where(lane < E // 2, low, high)

            return by_field(read)

        g_ref[...] += gather([pair(0), pair(2)], ohr_ref)
        for i in range(4):
            turn = turn_ref[i : i + 1, :]
            for_one, for_two = turn == 1, turn == 2
            totals = [x_ref[i * FACE_PAD : (i + 1) * FACE_PAD, cols(g)] for g in range(FIELDS)]
            for f in range(FIELDS):
                raw = g_ref[f * FACE_PAD : (f + 1) * FACE_PAD, cols(i)]
                v = [raw[c * 8 : (c + 1) * 8] for c in range(3)]
                y = jnp.concatenate(
                    [
                        jnp.where(
                            for_one, v[(c + 1) % 3], jnp.where(for_two, v[(c + 2) % 3], v[c])
                        )
                        for c in range(3)
                    ],
                    axis=0,
                )
                for g in range(FIELDS):
                    totals[g] = totals[g] + minus_ref[f, g, i : i + 1, :] * y
            for g in range(FIELDS):
                x_ref[i * FACE_PAD : (i + 1) * FACE_PAD, cols(g)] = totals[g]

    def lifted(group):
        for g in group:
            high, low = high_low(x_ref[:, cols(g)])
            r_ref[0:FACES, cols(g)] = high.astype(BF)
            r_ref[FACES : 2 * FACES, cols(g)] = low.astype(BF)
        both = dot(l_ref[...], r_ref[:, cols(group[0], len(group))])
        return [
            both[0:MODES, cols(n)] + both[MODES : 2 * MODES, cols(n)] for n in range(len(group))
        ]

    taylor_rest(False)
    copies = exchange(0)
    for f in range(FIELDS):
        base_ref[f] = sol_ref[f]
    local_part()
    remote_part(0, copies)
    for group in GROUPS:
        update = lifted(group)
        for n, g in enumerate(group):
            stepped = base_ref[g] - update[n]
            base_ref[g] = stepped
            prev_ref[g] = jnp.where(small, stepped, sol_ref[g])
    for group in GROUPS:
        for f in group:
            u = prev_ref[f]
            split_into(u, f)
            first_ref[f] = half[0] * u
        multiply(a_ref, 3 * MODES, group, 0)
    taylor_rest(True)
    copies = exchange(1)
    local_part()
    remote_part(1, copies)
    for group in GROUPS:
        update = lifted(group)
        for n, g in enumerate(group):
            out_ref[g] = base_ref[g] - update[n]


def on_device(
    n_dom,
    n_near,
    solution,
    star_matrices,
    flux_plus,
    flux_minus,
    stiffness,
    face_lift,
    face_project,
    cluster,
    neighbour_part,
    neighbour_slot,
    neighbour_face,
    orientation,
    halo_send,
):
    field_block = pltpu.VMEM((FIELDS, MODES, E), F32)
    step = pl.pallas_call(
        functools.partial(kernel, n_dom, n_near),
        out_shape=jax.ShapeDtypeStruct((FIELDS, MODES, E), F32),
        in_specs=[pl.BlockSpec(memory_space=pltpu.VMEM)] * 13,
        out_specs=pl.BlockSpec(memory_space=pltpu.VMEM),
        scratch_shapes=[
            pltpu.VMEM((3 * KPAD, COLS), BF),
            pltpu.VMEM((2, FACES + 3 * MODES, COLS), F32),
            field_block,
            field_block,
            field_block,
            pltpu.VMEM((FACES, COLS), F32),
            pltpu.VMEM((FIELDS * FACE_PAD, 4 * E), F32),
            field_block,
            pltpu.VMEM((3 * MODES, 3 * KPAD), BF),
            pltpu.VMEM((FACES + 3 * MODES, 3 * KPAD), BF),
            pltpu.VMEM((FACES, 3 * KPAD), BF),
            pltpu.VMEM((2 * MODES, 2 * FACES), BF),
            pltpu.VMEM((4 * E, 4 * E), BF),
            pltpu.VMEM((16 * HALO, 4 * E), BF),
            pltpu.VMEM((2 * E, 4 * E), BF),
            pltpu.VMEM((2, 4, KPAD, E), F32),
            pltpu.VMEM((2, 4, KPAD, E), F32),
            pltpu.SemaphoreType.DMA((2, 4)),
            pltpu.SemaphoreType.DMA((2, 4)),
        ],
        compiler_params=pltpu.CompilerParams(
            collective_id=0, has_side_effects=True, vmem_limit_bytes=40 * 2**20
        ),
        name="cluster_step",
    )
    out = step(
        jnp.transpose(solution, (1, 0, 2)),
        jnp.transpose(star_matrices, (1, 2, 0, 3)),
        jnp.transpose(flux_plus, (1, 2, 0, 3)),
        jnp.transpose(flux_minus, (1, 2, 0, 3)),
        stiffness,
        jnp.transpose(face_lift, (2, 0, 1)),
        jnp.transpose(face_project, (1, 0, 2)),
        cluster.reshape(1, E),
        neighbour_part,
        neighbour_slot,
        neighbour_face,
        orientation,
        halo_send,
    )
    return jnp.transpose(out, (1, 0, 2))


def solution(mesh):
    both = ("dom", "near")
    in_specs = (
        P(None, None, both),
        P(None, None, None, both),
        P(None, None, None, both),
        P(None, None, None, both),
        P(),
        P(),
        P(),
        P(both),
        P(None, both),
        P(None, both),
        P(None, both),
        P(None, both),
        P(None, both),
    )
    return jax.shard_map(
        functools.partial(on_device, mesh.shape["dom"], mesh.shape["near"]),
        mesh=mesh,
        in_specs=in_specs,
        out_specs=P(None, None, both),
        check_vma=False,
    )
```

```python
import functools
import math

import jax
import jax.numpy as jnp
from jax import lax
from jax.experimental import pallas as pl
from jax.experimental.pallas import tpu as pltpu
from jax.sharding import PartitionSpec as P

MESH = pl.DeviceIdType.MESH
MODES = 56
FIELDS = 9
FACE_MODES = 21
ORDER = 6
E = 128
HALO = 16
KPAD = 64
FACE_PAD = 24
FACES = 4 * FACE_PAD
COLS = FIELDS * E
GROUPS = ((0, 1), (2, 3), (4, 5), (6, 7), (8,))
BF = jnp.bfloat16
F32 = jnp.float32


def orbit_nodes():
    degree = ORDER - 1
    nodes = [(a, b, degree - a - b) for a in range(degree + 1) for b in range(degree + 1 - a)]
    number = {node: n for n, node in enumerate(nodes)}
    seen, orbits = set(), []
    for node in nodes:
        if node in seen:
            continue
        a, b, c = node
        orbit = [(a, b, c), (b, c, a), (c, a, b)]
        seen.update(orbit)
        orbits.append([number[member] for member in orbit])
    order = [-1] * FACE_PAD
    for o, orbit in enumerate(orbits):
        for c in range(3):
            order[c * 8 + o] = orbit[c]
    return order


ORDERED = orbit_nodes()


def weights(begin, end):
    return [
        (end ** (k + 1) - begin ** (k + 1)) / math.factorial(k + 1) for k in range(ORDER)
    ]


def dot(a, b):
    return jnp.dot(a, b, preferred_element_type=F32)


def iota(shape, dim):
    return lax.broadcasted_iota(jnp.int32, shape, dim)


def ones_where(condition):
    return jnp.where(condition, 1.0, 0.0).astype(F32)


def high_low(x):
    high = x.astype(BF).astype(F32)
    return high, x - high


def place(x, marks):
    high, rest = high_low(x)
    middle, low = high_low(rest)
    marks = marks.astype(BF)
    return dot(high.astype(BF), marks) + dot(middle.astype(BF), marks) + dot(low.astype(BF), marks)


def place_left(marks, x):
    high, rest = high_low(x)
    middle, low = high_low(rest)
    marks = marks.astype(BF)
    return dot(marks, high.astype(BF)) + dot(marks, middle.astype(BF)) + dot(marks, low.astype(BF))


def threefold(matrix):
    high, low = high_low(matrix)
    row, col = iota((MODES, 3 * KPAD), 0), iota((MODES, 3 * KPAD), 1)
    twice = ones_where((col == row) | (col == row + KPAD)).astype(BF)
    last = ones_where(col == row + 2 * KPAD).astype(BF)
    return (dot(high.astype(BF), twice) + dot(low.astype(BF), last)).astype(BF)


def kernel(
    n_dom,
    n_near,
    *refs,
):
    sources, out_ref, held = refs[:13], refs[13], refs[14:27]
    (
        sol_ref,
        star_ref,
        plus_ref,
        minus_ref,
        stiff_ref,
        lift_ref,
        proj_ref,
        cluster_ref,
        part_ref,
        slot_ref,
        nface_ref,
        turn_ref,
        halo_ref,
    ) = held
    (
        r_ref,
        y_ref,
        first_ref,
        second_ref,
        base_ref,
        x_ref,
        g_ref,
        prev_ref,
        a_ref,
        b_ref,
        p_ref,
        l_ref,
        ohl_ref,
        ohr_ref,
        ohs_ref,
        send_buf,
        recv_buf,
        send_sem,
        recv_sem,
        load_sem,
    ) = refs[27:]
    loads = [
        pltpu.make_async_copy(source, target, load_sem.at[n])
        for n, (source, target) in enumerate(zip(sources, held))
    ]
    for n in (4, 0, 1, 12, 7, 8, 9, 10, 5, 6, 2, 3, 11):
        loads[n].start()
    dom, near = lax.axis_index("dom"), lax.axis_index("near")
    targets = (
        (dom, lax.rem(near + 1, n_near)),
        (dom, lax.rem(near + n_near - 1, n_near)),
        (lax.rem(dom + 1, n_dom), near),
        (lax.rem(dom + n_dom - 1, n_dom), near),
    )
    barrier = pltpu.get_barrier_semaphore()
    for target in targets:
        pl.semaphore_signal(barrier, inc=1, device_id=target, device_id_type=MESH)

    def cols(f, count=1):
        return slice(f * E, (f + count) * E)

    loads[4].wait()
    stiff = jnp.concatenate([stiff_ref[d] for d in range(3)], axis=0)
    a_ref[...] = threefold(stiff)

    def split_into(t, f):
        high, low = high_low(t)
        zero = jnp.zeros((KPAD - MODES, E), F32)
        high = jnp.concatenate([high, zero], axis=0).astype(BF)
        low = jnp.concatenate([low, zero], axis=0).astype(BF)
        r_ref[0:KPAD, cols(f)] = high
        r_ref[KPAD : 2 * KPAD, cols(f)] = low
        r_ref[2 * KPAD : 3 * KPAD, cols(f)] = high

    def multiply(matrix, rows, group, slot):
        span = cols(group[0], len(group))
        y_ref[slot, 0:rows, span] = dot(matrix[...], r_ref[:, span])

    def star(group, slot, row0=0):
        totals = [None] * len(group)
        for d in range(3):
            for f in range(FIELDS):
                y = y_ref[slot, row0 + d * MODES : row0 + (d + 1) * MODES, cols(f)]
                for n, g in enumerate(group):
                    term = star_ref[f, g, d : d + 1, :] * y
                    totals[n] = term if totals[n] is None else totals[n] + term
        return totals

    half, rest = weights(0.0, 0.5), weights(0.5, 1.0)

    loads[0].wait()
    for group in GROUPS:
        for f in group:
            u = sol_ref[f]
            split_into(u, f)
            first_ref[f] = half[0] * u
            second_ref[f] = rest[0] * u
        multiply(a_ref, 3 * MODES, group, 0)

    for n in (1, 12, 7, 8, 9, 10, 5, 6):
        loads[n].wait()
    small = cluster_ref[...] == 0
    backward = jnp.concatenate([stiff_ref[d].T for d in range(3)], axis=0)
    node, entry = iota((FACE_PAD, FACE_MODES), 1), iota((FACE_PAD, FACE_MODES), 0)
    chosen = entry < 0
    for spot, number in enumerate(ORDERED):
        if number >= 0:
            chosen = chosen | ((entry == spot) & (node == number))
    chosen = ones_where(chosen)
    project = jnp.concatenate([place_left(chosen, proj_ref[:, j, :]) for j in range(4)], axis=0)
    lifts = jnp.concatenate([place_left(chosen, lift_ref[:, j, :]) for j in range(4)], axis=0)
    b_ref[...] = threefold(jnp.concatenate([project, backward], axis=0))
    p_ref[...] = threefold(project)
    lift_high, lift_low = high_low(lifts.T)
    row, col = iota((FACES, 2 * FACES), 0), iota((FACES, 2 * FACES), 1)
    twice = ones_where((col == row) | (col == row + FACES)).astype(BF)
    once = ones_where(col == row).astype(BF)
    l_ref[...] = jnp.concatenate(
        [dot(lift_high.astype(BF), twice), dot(lift_low.astype(BF), once)], axis=0
    ).astype(BF)

    part, slot_of = part_ref[...], slot_ref[...]
    face_of = nface_ref[...]
    local_key = jnp.where(part == 0, face_of * E + slot_of, -1)
    remote_key = jnp.where(part > 0, face_of * (4 * HALO) + (part - 1) * HALO + slot_of, -1)
    for i in range(4):
        ohl_ref[:, cols(i)] = ones_where(local_key[i : i + 1, :] == iota((4 * E, E), 0)).astype(BF)
        ohr_ref[:, cols(i)] = ones_where(
            remote_key[i : i + 1, :] == iota((16 * HALO, E), 0)
        ).astype(BF)
    spread = ones_where(iota((HALO, E), 0) == lax.rem(iota((HALO, E), 1), HALO)).astype(BF)
    sent = dot(halo_ref[...].astype(F32).astype(BF), spread)
    for r in range(4):
        ohs_ref[:, cols(r)] = ones_where(
            sent[r : r + 1, :] == iota((2 * E, E), 0).astype(F32)
        ).astype(BF) + ones_where(
            sent[r : r + 1, :] + float(E) == iota((2 * E, E), 0).astype(F32)
        ).astype(BF)

    lane = iota((1, E), 1)
    lane_group = lane // HALO

    def taylor_rest(first_only):
        for k in range(ORDER - 2):
            for group in GROUPS:
                for g, t in zip(group, star(group, k % 2)):
                    split_into(t, g)
                    first_ref[g] += half[k + 1] * t
                    if not first_only:
                        second_ref[g] += rest[k + 1] * t
                multiply(a_ref, 3 * MODES, group, (k + 1) % 2)
        for group in GROUPS:
            for g, t in zip(group, star(group, 0)):
                value = first_ref[g] + half[5] * t
                if first_only:
                    value = jnp.where(small, value, second_ref[g])
                else:
                    second_ref[g] += rest[5] * t
                first_ref[g] = value

    def exchange(phase):
        copies = []
        highs, lows = [], []
        for f in range(FIELDS):
            high, low = high_low(first_ref[f])
            highs.append(high)
            lows.append(low)
        stacked = jnp.concatenate(
            [
                jnp.concatenate(highs, axis=0).astype(BF),
                jnp.concatenate(lows, axis=0).astype(BF),
            ],
            axis=1,
        )
        taken = dot(stacked, ohs_ref[...])
        for r in range(4):
            block = taken[:, cols(r)]
            packed = block[0:MODES]
            for f in range(1, 8):
                packed = jnp.where(lane_group == f, block[f * MODES : (f + 1) * MODES], packed)
            tail = block[8 * MODES : 8 * MODES + 8]
            for k in range(1, 7):
                start = 8 * MODES + 8 * k
                tail = jnp.where(lane_group == k, block[start : start + 8], tail)
            send_buf[phase, r] = jnp.concatenate([packed, tail], axis=0)
        if phase == 0:
            pl.semaphore_wait(barrier, 4)
        for r in range(4):
            copy = pltpu.make_async_remote_copy(
                src_ref=send_buf.at[phase, r],
                dst_ref=recv_buf.at[phase, r],
                send_sem=send_sem.at[phase, r],
                recv_sem=recv_sem.at[phase, r],
                device_id=targets[r],
                device_id_type=MESH,
            )
            copy.start()
            copies.append(copy)
        return copies

    def gather(blocks, marks):
        sides = []
        for block in blocks:
            high, low = high_low(block)
            sides.append(jnp.concatenate([high, low], axis=0).astype(BF))
        both = dot(jnp.concatenate(sides, axis=1), marks[...])
        rows = FIELDS * FACE_PAD
        return both[0:rows] + both[rows : 2 * rows]

    def by_field(read):
        return jnp.concatenate([read(f) for f in range(FIELDS)], axis=0)

    def local_part():
        for group in GROUPS:
            for f in group:
                split_into(first_ref[f], f)
            multiply(b_ref, FACES + 3 * MODES, group, 0)
        g_ref[...] = gather(
            [
                by_field(lambda f: y_ref[0, j * FACE_PAD : (j + 1) * FACE_PAD, cols(f)])
                for j in range(4)
            ],
            ohl_ref,
        )
        for i in range(4):
            totals = [None] * FIELDS
            for f in range(FIELDS):
                y = y_ref[0, i * FACE_PAD : (i + 1) * FACE_PAD, cols(f)]
                for g in range(FIELDS):
                    term = plus_ref[f, g, i : i + 1, :] * y
                    totals[g] = term if totals[g] is None else totals[g] + term
            for g in range(FIELDS):
                x_ref[i * FACE_PAD : (i + 1) * FACE_PAD, cols(g)] = totals[g]
        for group in GROUPS:
            for g, v in zip(group, star(group, 0, FACES)):
                base_ref[g] += v

    def remote_part(phase, copies):
        for copy in copies:
            copy.wait()
        rolled = []
        for r in range(4):
            block = recv_buf[phase, r]
            rolled.append(
                [block if c == 0 else pltpu.roll(block, c * HALO, 1) for c in range(8)]
            )

        def collect(at, rows):
            value = None
            for spot in range(8):
                r = spot % 4
                piece = rolled[r][(spot - at) % 8][rows]
                value = piece if value is None else jnp.where(lane_group == spot, piece, value)
            return value

        for group in GROUPS:
            for f in group:
                if f < 8:
                    split_into(collect(f, slice(0, MODES)), f)
                else:
                    tiles = [collect(k, slice(MODES, MODES + 8)) for k in range(7)]
                    split_into(jnp.concatenate(tiles, axis=0), f)
            multiply(p_ref, FACES, group, 1)

        def pair(j):
            def read(f):
                low = y_ref[1, j * FACE_PAD : (j + 1) * FACE_PAD, cols(f)]
                high = y_ref[1, (j + 1) * FACE_PAD : (j + 2) * FACE_PAD, cols(f)]
                return jnp.where(lane < E // 2, low, high)

            return by_field(read)

        g_ref[...] += gather([pair(0), pair(2)], ohr_ref)
        for i in range(4):
            turn = turn_ref[i : i + 1, :]
            for_one, for_two = turn == 1, turn == 2
            totals = [x_ref[i * FACE_PAD : (i + 1) * FACE_PAD, cols(g)] for g in range(FIELDS)]
            for f in range(FIELDS):
                raw = g_ref[f * FACE_PAD : (f + 1) * FACE_PAD, cols(i)]
                v = [raw[c * 8 : (c + 1) * 8] for c in range(3)]
                y = jnp.concatenate(
                    [
                        jnp.where(
                            for_one, v[(c + 1) % 3], jnp.where(for_two, v[(c + 2) % 3], v[c])
                        )
                        for c in range(3)
                    ],
                    axis=0,
                )
                for g in range(FIELDS):
                    totals[g] = totals[g] + minus_ref[f, g, i : i + 1, :] * y
            for g in range(FIELDS):
                x_ref[i * FACE_PAD : (i + 1) * FACE_PAD, cols(g)] = totals[g]

    def lifted(group):
        for g in group:
            high, low = high_low(x_ref[:, cols(g)])
            r_ref[0:FACES, cols(g)] = high.astype(BF)
            r_ref[FACES : 2 * FACES, cols(g)] = low.astype(BF)
        both = dot(l_ref[...], r_ref[:, cols(group[0], len(group))])
        return [
            both[0:MODES, cols(n)] + both[MODES : 2 * MODES, cols(n)] for n in range(len(group))
        ]

    taylor_rest(False)
    copies = exchange(0)
    for n in (2, 3, 11):
        loads[n].wait()
    for f in range(FIELDS):
        base_ref[f] = sol_ref[f]
    local_part()
    remote_part(0, copies)
    for group in GROUPS:
        update = lifted(group)
        for n, g in enumerate(group):
            stepped = base_ref[g] - update[n]
            base_ref[g] = stepped
            prev_ref[g] = jnp.where(small, stepped, sol_ref[g])
    for group in GROUPS:
        for f in group:
            u = prev_ref[f]
            split_into(u, f)
            first_ref[f] = half[0] * u
        multiply(a_ref, 3 * MODES, group, 0)
    taylor_rest(True)
    copies = exchange(1)
    local_part()
    remote_part(1, copies)
    for group in GROUPS:
        update = lifted(group)
        for n, g in enumerate(group):
            out_ref[g] = base_ref[g] - update[n]


def on_device(
    n_dom,
    n_near,
    solution,
    star_matrices,
    flux_plus,
    flux_minus,
    stiffness,
    face_lift,
    face_project,
    cluster,
    neighbour_part,
    neighbour_slot,
    neighbour_face,
    orientation,
    halo_send,
):
    operands = (
        jnp.transpose(solution, (1, 0, 2)),
        jnp.transpose(star_matrices, (1, 2, 0, 3)),
        jnp.transpose(flux_plus, (1, 2, 0, 3)),
        jnp.transpose(flux_minus, (1, 2, 0, 3)),
        stiffness,
        jnp.transpose(face_lift, (2, 0, 1)),
        jnp.transpose(face_project, (1, 0, 2)),
        cluster.reshape(1, E),
        neighbour_part,
        neighbour_slot,
        neighbour_face,
        orientation,
        halo_send,
    )
    field_block = pltpu.VMEM((FIELDS, MODES, E), F32)
    step = pl.pallas_call(
        functools.partial(kernel, n_dom, n_near),
        out_shape=jax.ShapeDtypeStruct((FIELDS, MODES, E), F32),
        in_specs=[pl.BlockSpec(memory_space=pltpu.HBM)] * 13,
        out_specs=pl.BlockSpec(memory_space=pltpu.VMEM),
        scratch_shapes=[pltpu.VMEM(value.shape, value.dtype) for value in operands]
        + [
            pltpu.VMEM((3 * KPAD, COLS), BF),
            pltpu.VMEM((2, FACES + 3 * MODES, COLS), F32),
            field_block,
            field_block,
            field_block,
            pltpu.VMEM((FACES, COLS), F32),
            pltpu.VMEM((FIELDS * FACE_PAD, 4 * E), F32),
            field_block,
            pltpu.VMEM((3 * MODES, 3 * KPAD), BF),
            pltpu.VMEM((FACES + 3 * MODES, 3 * KPAD), BF),
            pltpu.VMEM((FACES, 3 * KPAD), BF),
            pltpu.VMEM((2 * MODES, 2 * FACES), BF),
            pltpu.VMEM((4 * E, 4 * E), BF),
            pltpu.VMEM((16 * HALO, 4 * E), BF),
            pltpu.VMEM((2 * E, 4 * E), BF),
            pltpu.VMEM((2, 4, KPAD, E), F32),
            pltpu.VMEM((2, 4, KPAD, E), F32),
            pltpu.SemaphoreType.DMA((2, 4)),
            pltpu.SemaphoreType.DMA((2, 4)),
            pltpu.SemaphoreType.DMA((13,)),
        ],
        compiler_params=pltpu.CompilerParams(
            collective_id=0, has_side_effects=True, vmem_limit_bytes=60 * 2**20
        ),
        name="cluster_step",
    )
    out = step(*operands)
    return jnp.transpose(out, (1, 0, 2))


def solution(mesh):
    both = ("dom", "near")
    in_specs = (
        P(None, None, both),
        P(None, None, None, both),
        P(None, None, None, both),
        P(None, None, None, both),
        P(),
        P(),
        P(),
        P(both),
        P(None, both),
        P(None, both),
        P(None, both),
        P(None, both),
        P(None, both),
    )
    return jax.shard_map(
        functools.partial(on_device, mesh.shape["dom"], mesh.shape["near"]),
        mesh=mesh,
        in_specs=in_specs,
        out_specs=P(None, None, both),
        check_vma=False,
    )
```

```python
import functools
import math

import jax
import jax.numpy as jnp
from jax import lax
from jax.experimental import pallas as pl
from jax.experimental.pallas import tpu as pltpu
from jax.sharding import PartitionSpec as P

MESH = pl.DeviceIdType.MESH
MODES = 56
FIELDS = 9
FACE_MODES = 21
ORDER = 6
E = 128
HALO = 16
PACK = 64
PAIRS = ((0, 1), (2, 3), (4, 5), (6, 7), (8,))
PAIR_GROUPS = ((0, 1), (2, 3), (4,))
KPAD = 64
FACE_PAD = 24
FACES = 4 * FACE_PAD
COLS = FIELDS * E
GROUPS = ((0, 1), (2, 3), (4, 5), (6, 7), (8,))
BF = jnp.bfloat16
F32 = jnp.float32


def orbit_nodes():
    degree = ORDER - 1
    nodes = [(a, b, degree - a - b) for a in range(degree + 1) for b in range(degree + 1 - a)]
    number = {node: n for n, node in enumerate(nodes)}
    seen, orbits = set(), []
    for node in nodes:
        if node in seen:
            continue
        a, b, c = node
        orbit = [(a, b, c), (b, c, a), (c, a, b)]
        seen.update(orbit)
        orbits.append([number[member] for member in orbit])
    order = [-1] * FACE_PAD
    for o, orbit in enumerate(orbits):
        for c in range(3):
            order[c * 8 + o] = orbit[c]
    return order


ORDERED = orbit_nodes()


def weights(begin, end):
    return [
        (end ** (k + 1) - begin ** (k + 1)) / math.factorial(k + 1) for k in range(ORDER)
    ]


def dot(a, b):
    return jnp.dot(a, b, preferred_element_type=F32)


def iota(shape, dim):
    return lax.broadcasted_iota(jnp.int32, shape, dim)


def ones_where(condition):
    return jnp.where(condition, 1.0, 0.0).astype(F32)


def high_low(x):
    high = x.astype(BF).astype(F32)
    return high, x - high


def place(x, marks):
    high, rest = high_low(x)
    middle, low = high_low(rest)
    marks = marks.astype(BF)
    return dot(high.astype(BF), marks) + dot(middle.astype(BF), marks) + dot(low.astype(BF), marks)


def place_left(marks, x):
    high, rest = high_low(x)
    middle, low = high_low(rest)
    marks = marks.astype(BF)
    return dot(marks, high.astype(BF)) + dot(marks, middle.astype(BF)) + dot(marks, low.astype(BF))


def threefold(matrix):
    high, low = high_low(matrix)
    row, col = iota((MODES, 3 * KPAD), 0), iota((MODES, 3 * KPAD), 1)
    twice = ones_where((col == row) | (col == row + KPAD)).astype(BF)
    last = ones_where(col == row + 2 * KPAD).astype(BF)
    return (dot(high.astype(BF), twice) + dot(low.astype(BF), last)).astype(BF)


def kernel(
    n_dom,
    n_near,
    *refs,
):
    sources, out_ref, held = refs[:13], refs[13], refs[14:27]
    (
        sol_ref,
        star_ref,
        plus_ref,
        minus_ref,
        stiff_ref,
        lift_ref,
        proj_ref,
        cluster_ref,
        part_ref,
        slot_ref,
        nface_ref,
        turn_ref,
        halo_ref,
    ) = held
    (
        r_ref,
        y_ref,
        first_ref,
        second_ref,
        base_ref,
        x_ref,
        g_ref,
        a_ref,
        b_ref,
        p_ref,
        l_ref,
        ohl_ref,
        ohr_ref,
        ohs_ref,
        send_buf,
        recv_buf,
        send_sem,
        recv_sem,
        load_sem,
        star8_ref,
        packed_star_ref,
        compact_ref,
        widen_ref,
        j_ref,
    ) = refs[27:]
    loads = [
        pltpu.make_async_copy(source, target, load_sem.at[n])
        for n, (source, target) in enumerate(zip(sources, held))
    ]
    for n in (4, 0, 1, 12, 7, 8, 9, 10, 5, 6, 2, 3, 11):
        loads[n].start()
    dom, near = lax.axis_index("dom"), lax.axis_index("near")
    targets = (
        (dom, lax.rem(near + 1, n_near)),
        (dom, lax.rem(near + n_near - 1, n_near)),
        (lax.rem(dom + 1, n_dom), near),
        (lax.rem(dom + n_dom - 1, n_dom), near),
    )
    barrier = pltpu.get_barrier_semaphore()
    for target in targets:
        pl.semaphore_signal(barrier, inc=1, device_id=target, device_id_type=MESH)

    def cols(f, count=1):
        return slice(f * E, (f + count) * E)

    loads[4].wait()
    stiff = jnp.concatenate([stiff_ref[d] for d in range(3)], axis=0)
    a_ref[...] = threefold(stiff)

    def split_into(t, f):
        high, low = high_low(t)
        zero = jnp.zeros((KPAD - MODES, E), F32)
        high = jnp.concatenate([high, zero], axis=0).astype(BF)
        low = jnp.concatenate([low, zero], axis=0).astype(BF)
        r_ref[0:KPAD, cols(f)] = high
        r_ref[KPAD : 2 * KPAD, cols(f)] = low
        r_ref[2 * KPAD : 3 * KPAD, cols(f)] = high

    def multiply(matrix, rows, group, slot):
        span = cols(group[0], len(group))
        y_ref[slot, 0:rows, span] = dot(matrix[...], r_ref[:, span])

    def spread_mul(tile, y):
        return (tile[None] * y.reshape(MODES // 8, 8, E)).reshape(MODES, E)

    def star(group, slot, row0=0):
        totals = [None] * len(group)
        for d in range(3):
            for f in range(FIELDS):
                y = y_ref[slot, row0 + d * MODES : row0 + (d + 1) * MODES, cols(f)]
                for n, g in enumerate(group):
                    term = spread_mul(star8_ref[f, g, d], y)
                    totals[n] = term if totals[n] is None else totals[n] + term
        return totals

    half, rest = weights(0.0, 0.5), weights(0.5, 1.0)

    loads[0].wait()
    for group in GROUPS:
        for f in group:
            u = sol_ref[f]
            split_into(u, f)
            first_ref[f] = half[0] * u
            second_ref[f] = rest[0] * u
        multiply(a_ref, 3 * MODES, group, 0)

    for n in (1, 12, 7, 8, 9, 10, 5, 6):
        loads[n].wait()
    small = cluster_ref[...] == 0
    for f in range(FIELDS):
        for g in range(FIELDS):
            for d in range(3):
                star8_ref[f, g, d] = jnp.broadcast_to(star_ref[f, g, d : d + 1, :], (8, E))
    before = ones_where(iota((E, E), 0) < iota((E, E), 1)).astype(BF)
    small_row = ones_where(small)
    rank_row = dot(jnp.broadcast_to(small_row, (8, E)).astype(BF), before)[0:1]
    rank_row = jnp.where(small, rank_row, -1.0)
    square = iota((E, E), 0) == iota((E, E), 1)
    rank_col = jnp.sum(jnp.where(square, rank_row, 0.0), axis=1, keepdims=True)
    place_of = lax.rem(iota((E, E), 1), PACK).astype(F32)
    compact = ones_where(rank_col == place_of).astype(BF)
    compact_ref[0:E] = compact
    compact_ref[E : 2 * E] = compact
    source = iota((E, E), 0)
    for h in range(2):
        wide = ones_where(rank_row == (source - h * PACK).astype(F32)).astype(BF)
        widen_ref[0:E, cols(h)] = wide
        widen_ref[E : 2 * E, cols(h)] = wide
    backward = jnp.concatenate([stiff_ref[d].T for d in range(3)], axis=0)
    node, entry = iota((FACE_PAD, FACE_MODES), 1), iota((FACE_PAD, FACE_MODES), 0)
    chosen = entry < 0
    for spot, number in enumerate(ORDERED):
        if number >= 0:
            chosen = chosen | ((entry == spot) & (node == number))
    chosen = ones_where(chosen)
    project = jnp.concatenate([place_left(chosen, proj_ref[:, j, :]) for j in range(4)], axis=0)
    lifts = jnp.concatenate([place_left(chosen, lift_ref[:, j, :]) for j in range(4)], axis=0)
    b_ref[...] = threefold(jnp.concatenate([project, backward], axis=0))
    p_ref[...] = threefold(project)
    lift_high, lift_low = high_low(lifts.T)
    row, col = iota((FACES, 2 * FACES), 0), iota((FACES, 2 * FACES), 1)
    twice = ones_where((col == row) | (col == row + FACES)).astype(BF)
    once = ones_where(col == row).astype(BF)
    l_ref[...] = jnp.concatenate(
        [dot(lift_high.astype(BF), twice), dot(lift_low.astype(BF), once)], axis=0
    ).astype(BF)

    part, slot_of = part_ref[...], slot_ref[...]
    face_of = nface_ref[...]
    local_key = jnp.where(part == 0, face_of * E + slot_of, -1)
    remote_key = jnp.where(part > 0, face_of * (4 * HALO) + (part - 1) * HALO + slot_of, -1)
    for i in range(4):
        ohl_ref[:, cols(i)] = ones_where(local_key[i : i + 1, :] == iota((4 * E, E), 0)).astype(BF)
        ohr_ref[:, cols(i)] = ones_where(
            remote_key[i : i + 1, :] == iota((16 * HALO, E), 0)
        ).astype(BF)
    spread = ones_where(iota((HALO, E), 0) == lax.rem(iota((HALO, E), 1), HALO)).astype(BF)
    sent = dot(halo_ref[...].astype(F32).astype(BF), spread)
    for r in range(4):
        ohs_ref[:, cols(r)] = ones_where(
            sent[r : r + 1, :] == iota((2 * E, E), 0).astype(F32)
        ).astype(BF) + ones_where(
            sent[r : r + 1, :] + float(E) == iota((2 * E, E), 0).astype(F32)
        ).astype(BF)

    lane = iota((1, E), 1)
    lane_group = lane // HALO

    def first_stack():
        for k in range(ORDER - 2):
            for group in GROUPS:
                for g, t in zip(group, star(group, k % 2)):
                    split_into(t, g)
                    first_ref[g] += half[k + 1] * t
                    second_ref[g] += rest[k + 1] * t
                multiply(a_ref, 3 * MODES, group, (k + 1) % 2)
        for group in GROUPS:
            for g, t in zip(group, star(group, 0)):
                first_ref[g] += half[5] * t
                second_ref[g] += rest[5] * t

    lower = lane < PACK

    def sides(block):
        high, low = high_low(block)
        return jnp.concatenate([high.astype(BF), low.astype(BF)], axis=1)

    def pack_star():
        rows = FIELDS * 3 * 8
        for p, pair in enumerate(PAIRS):
            taken = [
                dot(sides(star8_ref[f].reshape(rows, E)), compact_ref[...]) for f in pair
            ]
            both = jnp.where(lower, taken[0], taken[1] if len(pair) == 2 else 0.0)
            packed_star_ref[p] = both.reshape(FIELDS, 3, 8, E)

    def packed_star(pairs, slot):
        fields = [g for p in pairs for g in PAIRS[p]]
        totals = dict.fromkeys(fields)
        for d in range(3):
            for q in range(len(PAIRS)):
                y = y_ref[slot, d * MODES : (d + 1) * MODES, cols(q)]
                for g in fields:
                    term = spread_mul(packed_star_ref[q, g, d], y)
                    totals[g] = term if totals[g] is None else totals[g] + term
        folded = []
        for p in pairs:
            one = totals[PAIRS[p][0]]
            if len(PAIRS[p]) == 2:
                two = totals[PAIRS[p][1]]
                folded.append(
                    jnp.where(lower, one, two) + pltpu.roll(jnp.where(lower, two, one), PACK, 1)
                )
            else:
                folded.append(jnp.where(lower, one + pltpu.roll(one, PACK, 1), 0.0))
        return folded

    def second_stack():
        for group in PAIR_GROUPS:
            for p in group:
                taken = [dot(sides(base_ref[f]), compact_ref[...]) for f in PAIRS[p]]
                u = jnp.where(lower, taken[0], taken[1] if len(taken) == 2 else 0.0)
                split_into(u, p)
                j_ref[p] = half[0] * u
            multiply(a_ref, 3 * MODES, group, 0)
        for k in range(ORDER - 2):
            for group in PAIR_GROUPS:
                for p, t in zip(group, packed_star(group, k % 2)):
                    split_into(t, p)
                    j_ref[p] += half[k + 1] * t
                multiply(a_ref, 3 * MODES, group, (k + 1) % 2)
        for group in PAIR_GROUPS:
            for p, t in zip(group, packed_star(group, 0)):
                wide = dot(sides(j_ref[p] + half[5] * t), widen_ref[...])
                for n, f in enumerate(PAIRS[p]):
                    first_ref[f] = jnp.where(small, wide[:, cols(n)], second_ref[f])

    def exchange(phase):
        copies = []
        highs, lows = [], []
        for f in range(FIELDS):
            high, low = high_low(first_ref[f])
            highs.append(high)
            lows.append(low)
        stacked = jnp.concatenate(
            [
                jnp.concatenate(highs, axis=0).astype(BF),
                jnp.concatenate(lows, axis=0).astype(BF),
            ],
            axis=1,
        )
        taken = dot(stacked, ohs_ref[...])
        for r in range(4):
            block = taken[:, cols(r)]
            packed = block[0:MODES]
            for f in range(1, 8):
                packed = jnp.where(lane_group == f, block[f * MODES : (f + 1) * MODES], packed)
            tail = block[8 * MODES : 8 * MODES + 8]
            for k in range(1, 7):
                start = 8 * MODES + 8 * k
                tail = jnp.where(lane_group == k, block[start : start + 8], tail)
            send_buf[phase, r] = jnp.concatenate([packed, tail], axis=0)
        if phase == 0:
            pl.semaphore_wait(barrier, 4)
        for r in range(4):
            copy = pltpu.make_async_remote_copy(
                src_ref=send_buf.at[phase, r],
                dst_ref=recv_buf.at[phase, r],
                send_sem=send_sem.at[phase, r],
                recv_sem=recv_sem.at[phase, r],
                device_id=targets[r],
                device_id_type=MESH,
            )
            copy.start()
            copies.append(copy)
        return copies

    def gather(blocks, marks):
        sides = []
        for block in blocks:
            high, low = high_low(block)
            sides.append(jnp.concatenate([high, low], axis=0).astype(BF))
        both = dot(jnp.concatenate(sides, axis=1), marks[...])
        rows = FIELDS * FACE_PAD
        return both[0:rows] + both[rows : 2 * rows]

    def by_field(read):
        return jnp.concatenate([read(f) for f in range(FIELDS)], axis=0)

    def local_part():
        for group in GROUPS:
            for f in group:
                split_into(first_ref[f], f)
            multiply(b_ref, FACES + 3 * MODES, group, 0)
        g_ref[...] = gather(
            [
                by_field(lambda f: y_ref[0, j * FACE_PAD : (j + 1) * FACE_PAD, cols(f)])
                for j in range(4)
            ],
            ohl_ref,
        )
        for i in range(4):
            totals = [None] * FIELDS
            for f in range(FIELDS):
                y = y_ref[0, i * FACE_PAD : (i + 1) * FACE_PAD, cols(f)]
                for g in range(FIELDS):
                    term = plus_ref[f, g, i : i + 1, :] * y
                    totals[g] = term if totals[g] is None else totals[g] + term
            for g in range(FIELDS):
                x_ref[i * FACE_PAD : (i + 1) * FACE_PAD, cols(g)] = totals[g]
        for group in GROUPS:
            for g, v in zip(group, star(group, 0, FACES)):
                base_ref[g] += v

    def remote_part(phase, copies):
        for copy in copies:
            copy.wait()
        rolled = []
        for r in range(4):
            block = recv_buf[phase, r]
            rolled.append(
                [block if c == 0 else pltpu.roll(block, c * HALO, 1) for c in range(8)]
            )

        def collect(at, rows):
            value = None
            for spot in range(8):
                r = spot % 4
                piece = rolled[r][(spot - at) % 8][rows]
                value = piece if value is None else jnp.where(lane_group == spot, piece, value)
            return value

        for group in GROUPS:
            for f in group:
                if f < 8:
                    split_into(collect(f, slice(0, MODES)), f)
                else:
                    tiles = [collect(k, slice(MODES, MODES + 8)) for k in range(7)]
                    split_into(jnp.concatenate(tiles, axis=0), f)
            multiply(p_ref, FACES, group, 1)

        def pair(j):
            def read(f):
                low = y_ref[1, j * FACE_PAD : (j + 1) * FACE_PAD, cols(f)]
                high = y_ref[1, (j + 1) * FACE_PAD : (j + 2) * FACE_PAD, cols(f)]
                return jnp.where(lane < E // 2, low, high)

            return by_field(read)

        g_ref[...] += gather([pair(0), pair(2)], ohr_ref)
        for i in range(4):
            turn = turn_ref[i : i + 1, :]
            for_one, for_two = turn == 1, turn == 2
            totals = [x_ref[i * FACE_PAD : (i + 1) * FACE_PAD, cols(g)] for g in range(FIELDS)]
            for f in range(FIELDS):
                raw = g_ref[f * FACE_PAD : (f + 1) * FACE_PAD, cols(i)]
                v = [raw[c * 8 : (c + 1) * 8] for c in range(3)]
                y = jnp.concatenate(
                    [
                        jnp.where(
                            for_one, v[(c + 1) % 3], jnp.where(for_two, v[(c + 2) % 3], v[c])
                        )
                        for c in range(3)
                    ],
                    axis=0,
                )
                for g in range(FIELDS):
                    totals[g] = totals[g] + minus_ref[f, g, i : i + 1, :] * y
            for g in range(FIELDS):
                x_ref[i * FACE_PAD : (i + 1) * FACE_PAD, cols(g)] = totals[g]

    def lifted(group):
        for g in group:
            high, low = high_low(x_ref[:, cols(g)])
            r_ref[0:FACES, cols(g)] = high.astype(BF)
            r_ref[FACES : 2 * FACES, cols(g)] = low.astype(BF)
        both = dot(l_ref[...], r_ref[:, cols(group[0], len(group))])
        return [
            both[0:MODES, cols(n)] + both[MODES : 2 * MODES, cols(n)] for n in range(len(group))
        ]

    first_stack()
    copies = exchange(0)
    for n in (2, 3, 11):
        loads[n].wait()
    for f in range(FIELDS):
        base_ref[f] = sol_ref[f]
    pack_star()
    local_part()
    remote_part(0, copies)
    for group in GROUPS:
        update = lifted(group)
        for n, g in enumerate(group):
            base_ref[g] -= update[n]
    second_stack()
    copies = exchange(1)
    local_part()
    remote_part(1, copies)
    for group in GROUPS:
        update = lifted(group)
        for n, g in enumerate(group):
            out_ref[g] = base_ref[g] - update[n]


def on_device(
    n_dom,
    n_near,
    solution,
    star_matrices,
    flux_plus,
    flux_minus,
    stiffness,
    face_lift,
    face_project,
    cluster,
    neighbour_part,
    neighbour_slot,
    neighbour_face,
    orientation,
    halo_send,
):
    operands = (
        jnp.transpose(solution, (1, 0, 2)),
        jnp.transpose(star_matrices, (1, 2, 0, 3)),
        jnp.transpose(flux_plus, (1, 2, 0, 3)),
        jnp.transpose(flux_minus, (1, 2, 0, 3)),
        stiffness,
        jnp.transpose(face_lift, (2, 0, 1)),
        jnp.transpose(face_project, (1, 0, 2)),
        cluster.reshape(1, E),
        neighbour_part,
        neighbour_slot,
        neighbour_face,
        orientation,
        halo_send,
    )
    field_block = pltpu.VMEM((FIELDS, MODES, E), F32)
    step = pl.pallas_call(
        functools.partial(kernel, n_dom, n_near),
        out_shape=pltpu.VMEM((FIELDS, MODES, E), F32),
        in_specs=[pl.BlockSpec(memory_space=pltpu.HBM)] * 13,
        out_specs=pl.BlockSpec(memory_space=pltpu.VMEM),
        scratch_shapes=[pltpu.VMEM(value.shape, value.dtype) for value in operands]
        + [
            pltpu.VMEM((3 * KPAD, COLS), BF),
            pltpu.VMEM((2, FACES + 3 * MODES, COLS), F32),
            field_block,
            field_block,
            field_block,
            pltpu.VMEM((FACES, COLS), F32),
            pltpu.VMEM((FIELDS * FACE_PAD, 4 * E), F32),
            pltpu.VMEM((3 * MODES, 3 * KPAD), BF),
            pltpu.VMEM((FACES + 3 * MODES, 3 * KPAD), BF),
            pltpu.VMEM((FACES, 3 * KPAD), BF),
            pltpu.VMEM((2 * MODES, 2 * FACES), BF),
            pltpu.VMEM((4 * E, 4 * E), BF),
            pltpu.VMEM((16 * HALO, 4 * E), BF),
            pltpu.VMEM((2 * E, 4 * E), BF),
            pltpu.VMEM((2, 4, KPAD, E), F32),
            pltpu.VMEM((2, 4, KPAD, E), F32),
            pltpu.SemaphoreType.DMA((2, 4)),
            pltpu.SemaphoreType.DMA((2, 4)),
            pltpu.SemaphoreType.DMA((13,)),
            pltpu.VMEM((FIELDS, FIELDS, 3, 8, E), F32),
            pltpu.VMEM((len(PAIRS), FIELDS, 3, 8, E), F32),
            pltpu.VMEM((2 * E, E), BF),
            pltpu.VMEM((2 * E, 2 * E), BF),
            pltpu.VMEM((len(PAIRS), MODES, E), F32),
        ],
        compiler_params=pltpu.CompilerParams(
            collective_id=0, has_side_effects=True, vmem_limit_bytes=60 * 2**20
        ),
        name="cluster_step",
    )
    out = step(*operands)
    return jnp.transpose(out, (1, 0, 2))


def solution(mesh):
    both = ("dom", "near")
    in_specs = (
        P(None, None, both),
        P(None, None, None, both),
        P(None, None, None, both),
        P(None, None, None, both),
        P(),
        P(),
        P(),
        P(both),
        P(None, both),
        P(None, both),
        P(None, both),
        P(None, both),
        P(None, both),
    )
    return jax.shard_map(
        functools.partial(on_device, mesh.shape["dom"], mesh.shape["near"]),
        mesh=mesh,
        in_specs=in_specs,
        out_specs=P(None, None, both),
        check_vma=False,
    )
```

```python
import functools
import math

import jax
import jax.numpy as jnp
from jax import lax
from jax.experimental import pallas as pl
from jax.experimental.pallas import tpu as pltpu
from jax.sharding import PartitionSpec as P

MESH = pl.DeviceIdType.MESH
MODES = 56
FIELDS = 9
FACE_MODES = 21
ORDER = 6
E = 128
HALO = 16
PACK = 64
PAIRS = ((0, 1), (2, 3), (4, 5), (6, 7), (8,))
PAIR_GROUPS = ((0, 1), (2, 3), (4,))
KPAD = 64
FACE_PAD = 24
FACES = 4 * FACE_PAD
COLS = FIELDS * E
GROUPS = ((0, 1), (2, 3), (4, 5), (6, 7), (8,))
BF = jnp.bfloat16
F32 = jnp.float32


def orbit_nodes():
    degree = ORDER - 1
    nodes = [(a, b, degree - a - b) for a in range(degree + 1) for b in range(degree + 1 - a)]
    number = {node: n for n, node in enumerate(nodes)}
    seen, orbits = set(), []
    for node in nodes:
        if node in seen:
            continue
        a, b, c = node
        orbit = [(a, b, c), (b, c, a), (c, a, b)]
        seen.update(orbit)
        orbits.append([number[member] for member in orbit])
    order = [-1] * FACE_PAD
    for o, orbit in enumerate(orbits):
        for c in range(3):
            order[c * 8 + o] = orbit[c]
    return order


ORDERED = orbit_nodes()


def weights(begin, end):
    return [
        (end ** (k + 1) - begin ** (k + 1)) / math.factorial(k + 1) for k in range(ORDER)
    ]


def dot(a, b):
    return jnp.dot(a, b, preferred_element_type=F32)


def iota(shape, dim):
    return lax.broadcasted_iota(jnp.int32, shape, dim)


def ones_where(condition):
    return jnp.where(condition, 1.0, 0.0).astype(F32)


def high_low(x):
    high = x.astype(BF).astype(F32)
    return high, x - high


def place(x, marks):
    high, rest = high_low(x)
    middle, low = high_low(rest)
    marks = marks.astype(BF)
    return dot(high.astype(BF), marks) + dot(middle.astype(BF), marks) + dot(low.astype(BF), marks)


def place_left(marks, x):
    high, rest = high_low(x)
    middle, low = high_low(rest)
    marks = marks.astype(BF)
    return dot(marks, high.astype(BF)) + dot(marks, middle.astype(BF)) + dot(marks, low.astype(BF))


def threefold(matrix):
    high, low = high_low(matrix)
    row, col = iota((MODES, 3 * KPAD), 0), iota((MODES, 3 * KPAD), 1)
    twice = ones_where((col == row) | (col == row + KPAD)).astype(BF)
    last = ones_where(col == row + 2 * KPAD).astype(BF)
    return (dot(high.astype(BF), twice) + dot(low.astype(BF), last)).astype(BF)


def kernel(
    n_dom,
    n_near,
    *refs,
):
    sources, out_ref, held = refs[:13], refs[13], refs[14:27]
    (
        sol_ref,
        star_ref,
        plus_ref,
        minus_ref,
        stiff_ref,
        lift_ref,
        proj_ref,
        cluster_ref,
        part_ref,
        slot_ref,
        nface_ref,
        turn_ref,
        halo_ref,
    ) = held
    (
        r_ref,
        y_ref,
        first_ref,
        second_ref,
        base_ref,
        x_ref,
        g_ref,
        a_ref,
        b_ref,
        p_ref,
        l_ref,
        ohl_ref,
        ohr_ref,
        ohs_ref,
        send_buf,
        recv_buf,
        send_sem,
        recv_sem,
        load_sem,
        star8_ref,
        packed_star_ref,
        compact_ref,
        widen_ref,
        j_ref,
    ) = refs[27:]
    loads = [
        pltpu.make_async_copy(source, target, load_sem.at[n])
        for n, (source, target) in enumerate(zip(sources, held))
    ]
    for n in (4, 0, 1, 12, 7, 8, 9, 10, 5, 6, 2, 3, 11):
        loads[n].start()
    dom, near = lax.axis_index("dom"), lax.axis_index("near")
    targets = (
        (dom, lax.rem(near + 1, n_near)),
        (dom, lax.rem(near + n_near - 1, n_near)),
        (lax.rem(dom + 1, n_dom), near),
        (lax.rem(dom + n_dom - 1, n_dom), near),
    )
    barrier = pltpu.get_barrier_semaphore()
    for target in targets:
        pl.semaphore_signal(barrier, inc=1, device_id=target, device_id_type=MESH)

    def cols(f, count=1):
        return slice(f * E, (f + count) * E)

    loads[4].wait()
    stiff = jnp.concatenate([stiff_ref[d] for d in range(3)], axis=0)
    a_ref[...] = threefold(stiff)

    def split_into(t, f):
        high, low = high_low(t)
        zero = jnp.zeros((KPAD - MODES, E), F32)
        high = jnp.concatenate([high, zero], axis=0).astype(BF)
        low = jnp.concatenate([low, zero], axis=0).astype(BF)
        r_ref[0:KPAD, cols(f)] = high
        r_ref[KPAD : 2 * KPAD, cols(f)] = low
        r_ref[2 * KPAD : 3 * KPAD, cols(f)] = high

    def multiply(matrix, rows, group, slot):
        span = cols(group[0], len(group))
        y_ref[slot, 0:rows, span] = dot(matrix[...], r_ref[:, span])

    def spread_mul(tile, y):
        return (tile[None] * y.reshape(MODES // 8, 8, E)).reshape(MODES, E)

    def star(group, slot, row0=0):
        totals = [None] * len(group)
        for d in range(3):
            for f in range(FIELDS):
                y = y_ref[slot, row0 + d * MODES : row0 + (d + 1) * MODES, cols(f)]
                for n, g in enumerate(group):
                    term = spread_mul(star8_ref[f, g, d], y)
                    totals[n] = term if totals[n] is None else totals[n] + term
        return totals

    half, rest = weights(0.0, 0.5), weights(0.5, 1.0)

    loads[0].wait()
    for group in GROUPS:
        for f in group:
            u = sol_ref[f]
            split_into(u, f)
            first_ref[f] = half[0] * u
            second_ref[f] = rest[0] * u
        multiply(a_ref, 3 * MODES, group, 0)

    for n in (1, 12):
        loads[n].wait()
    for f in range(FIELDS):
        for g in range(FIELDS):
            for d in range(3):
                star8_ref[f, g, d] = jnp.broadcast_to(star_ref[f, g, d : d + 1, :], (8, E))
    spread = ones_where(iota((HALO, E), 0) == lax.rem(iota((HALO, E), 1), HALO)).astype(BF)
    sent = dot(halo_ref[...].astype(F32).astype(BF), spread)
    for r in range(4):
        ohs_ref[:, cols(r)] = ones_where(
            sent[r : r + 1, :] == iota((2 * E, E), 0).astype(F32)
        ).astype(BF) + ones_where(
            sent[r : r + 1, :] + float(E) == iota((2 * E, E), 0).astype(F32)
        ).astype(BF)

    lane = iota((1, E), 1)
    lane_group = lane // HALO

    def first_stack():
        for k in range(ORDER - 2):
            for group in GROUPS:
                for g, t in zip(group, star(group, k % 2)):
                    split_into(t, g)
                    first_ref[g] += half[k + 1] * t
                    second_ref[g] += rest[k + 1] * t
                multiply(a_ref, 3 * MODES, group, (k + 1) % 2)
        for group in GROUPS:
            for g, t in zip(group, star(group, 0)):
                first_ref[g] += half[5] * t
                second_ref[g] += rest[5] * t

    def other_operators(small):
        backward = jnp.concatenate([stiff_ref[d].T for d in range(3)], axis=0)
        node, entry = iota((FACE_PAD, FACE_MODES), 1), iota((FACE_PAD, FACE_MODES), 0)
        chosen = entry < 0
        for spot, number in enumerate(ORDERED):
            if number >= 0:
                chosen = chosen | ((entry == spot) & (node == number))
        chosen = ones_where(chosen)
        project = jnp.concatenate([place_left(chosen, proj_ref[:, j, :]) for j in range(4)], axis=0)
        lifts = jnp.concatenate([place_left(chosen, lift_ref[:, j, :]) for j in range(4)], axis=0)
        b_ref[...] = threefold(jnp.concatenate([project, backward], axis=0))
        p_ref[...] = threefold(project)
        lift_high, lift_low = high_low(lifts.T)
        row, col = iota((FACES, 2 * FACES), 0), iota((FACES, 2 * FACES), 1)
        twice = ones_where((col == row) | (col == row + FACES)).astype(BF)
        once = ones_where(col == row).astype(BF)
        l_ref[...] = jnp.concatenate(
            [dot(lift_high.astype(BF), twice), dot(lift_low.astype(BF), once)], axis=0
        ).astype(BF)

        part, slot_of = part_ref[...], slot_ref[...]
        face_of = nface_ref[...]
        local_key = jnp.where(part == 0, face_of * E + slot_of, -1)
        remote_key = jnp.where(part > 0, face_of * (4 * HALO) + (part - 1) * HALO + slot_of, -1)
        for i in range(4):
            ohl_ref[:, cols(i)] = ones_where(local_key[i : i + 1, :] == iota((4 * E, E), 0)).astype(BF)
            ohr_ref[:, cols(i)] = ones_where(
                remote_key[i : i + 1, :] == iota((16 * HALO, E), 0)
            ).astype(BF)
        before = ones_where(iota((E, E), 0) < iota((E, E), 1)).astype(BF)
        small_row = ones_where(small)
        rank_row = dot(jnp.broadcast_to(small_row, (8, E)).astype(BF), before)[0:1]
        rank_row = jnp.where(small, rank_row, -1.0)
        square = iota((E, E), 0) == iota((E, E), 1)
        rank_col = jnp.sum(jnp.where(square, rank_row, 0.0), axis=1, keepdims=True)
        place_of = lax.rem(iota((E, E), 1), PACK).astype(F32)
        compact = ones_where(rank_col == place_of).astype(BF)
        compact_ref[0:E] = compact
        compact_ref[E : 2 * E] = compact
        source = iota((E, E), 0)
        for h in range(2):
            wide = ones_where(rank_row == (source - h * PACK).astype(F32)).astype(BF)
            widen_ref[0:E, cols(h)] = wide
            widen_ref[E : 2 * E, cols(h)] = wide

    lower = lane < PACK

    def sides(block):
        high, low = high_low(block)
        return jnp.concatenate([high.astype(BF), low.astype(BF)], axis=1)

    def pack_star():
        rows = FIELDS * 3 * 8
        for p, pair in enumerate(PAIRS):
            taken = [
                dot(sides(star8_ref[f].reshape(rows, E)), compact_ref[...]) for f in pair
            ]
            both = jnp.where(lower, taken[0], taken[1] if len(pair) == 2 else 0.0)
            packed_star_ref[p] = both.reshape(FIELDS, 3, 8, E)

    def packed_star(pairs, slot):
        fields = [g for p in pairs for g in PAIRS[p]]
        totals = dict.fromkeys(fields)
        for d in range(3):
            for q in range(len(PAIRS)):
                y = y_ref[slot, d * MODES : (d + 1) * MODES, cols(q)]
                for g in fields:
                    term = spread_mul(packed_star_ref[q, g, d], y)
                    totals[g] = term if totals[g] is None else totals[g] + term
        folded = []
        for p in pairs:
            one = totals[PAIRS[p][0]]
            if len(PAIRS[p]) == 2:
                two = totals[PAIRS[p][1]]
                folded.append(
                    jnp.where(lower, one, two) + pltpu.roll(jnp.where(lower, two, one), PACK, 1)
                )
            else:
                folded.append(jnp.where(lower, one + pltpu.roll(one, PACK, 1), 0.0))
        return folded

    def second_stack():
        for group in PAIR_GROUPS:
            for p in group:
                taken = [dot(sides(base_ref[f]), compact_ref[...]) for f in PAIRS[p]]
                u = jnp.where(lower, taken[0], taken[1] if len(taken) == 2 else 0.0)
                split_into(u, p)
                j_ref[p] = half[0] * u
            multiply(a_ref, 3 * MODES, group, 0)
        for k in range(ORDER - 2):
            for group in PAIR_GROUPS:
                for p, t in zip(group, packed_star(group, k % 2)):
                    split_into(t, p)
                    j_ref[p] += half[k + 1] * t
                multiply(a_ref, 3 * MODES, group, (k + 1) % 2)
        for group in PAIR_GROUPS:
            for p, t in zip(group, packed_star(group, 0)):
                wide = dot(sides(j_ref[p] + half[5] * t), widen_ref[...])
                for n, f in enumerate(PAIRS[p]):
                    first_ref[f] = jnp.where(small, wide[:, cols(n)], second_ref[f])

    def exchange(phase):
        copies = []
        highs, lows = [], []
        for f in range(FIELDS):
            high, low = high_low(first_ref[f])
            highs.append(high)
            lows.append(low)
        stacked = jnp.concatenate(
            [
                jnp.concatenate(highs, axis=0).astype(BF),
                jnp.concatenate(lows, axis=0).astype(BF),
            ],
            axis=1,
        )
        for pair in ((2, 3), (0, 1)):
            taken = dot(stacked, ohs_ref[:, cols(pair[0], 2)])
            for n, r in enumerate(pair):
                block = taken[:, cols(n)]
                packed = block[0:MODES]
                for f in range(1, 8):
                    packed = jnp.where(lane_group == f, block[f * MODES : (f + 1) * MODES], packed)
                tail = block[8 * MODES : 8 * MODES + 8]
                for k in range(1, 7):
                    start = 8 * MODES + 8 * k
                    tail = jnp.where(lane_group == k, block[start : start + 8], tail)
                send_buf[phase, r] = jnp.concatenate([packed, tail], axis=0)
            if phase == 0 and pair[0] == 2:
                pl.semaphore_wait(barrier, 4)
            for r in pair:
                copy = pltpu.make_async_remote_copy(
                    src_ref=send_buf.at[phase, r],
                    dst_ref=recv_buf.at[phase, r],
                    send_sem=send_sem.at[phase, r],
                    recv_sem=recv_sem.at[phase, r],
                    device_id=targets[r],
                    device_id_type=MESH,
                )
                copy.start()
                copies.append(copy)
        return copies

    def gather(blocks, marks):
        sides = []
        for block in blocks:
            high, low = high_low(block)
            sides.append(jnp.concatenate([high, low], axis=0).astype(BF))
        both = dot(jnp.concatenate(sides, axis=1), marks[...])
        rows = FIELDS * FACE_PAD
        return both[0:rows] + both[rows : 2 * rows]

    def by_field(read):
        return jnp.concatenate([read(f) for f in range(FIELDS)], axis=0)

    def local_part():
        for group in GROUPS:
            for f in group:
                split_into(first_ref[f], f)
            multiply(b_ref, FACES + 3 * MODES, group, 0)
        g_ref[...] = gather(
            [
                by_field(lambda f: y_ref[0, j * FACE_PAD : (j + 1) * FACE_PAD, cols(f)])
                for j in range(4)
            ],
            ohl_ref,
        )
        for i in range(4):
            totals = [None] * FIELDS
            for f in range(FIELDS):
                y = y_ref[0, i * FACE_PAD : (i + 1) * FACE_PAD, cols(f)]
                for g in range(FIELDS):
                    term = plus_ref[f, g, i : i + 1, :] * y
                    totals[g] = term if totals[g] is None else totals[g] + term
            for g in range(FIELDS):
                x_ref[i * FACE_PAD : (i + 1) * FACE_PAD, cols(g)] = totals[g]
        for group in GROUPS:
            for g, v in zip(group, star(group, 0, FACES)):
                base_ref[g] += v

    def remote_part(phase, copies):
        for copy in copies:
            copy.wait()
        rolled = []
        for r in range(4):
            block = recv_buf[phase, r]
            rolled.append(
                [block if c == 0 else pltpu.roll(block, c * HALO, 1) for c in range(8)]
            )

        def collect(at, rows):
            value = None
            for spot in range(8):
                r = spot % 4
                piece = rolled[r][(spot - at) % 8][rows]
                value = piece if value is None else jnp.where(lane_group == spot, piece, value)
            return value

        for group in GROUPS:
            for f in group:
                if f < 8:
                    split_into(collect(f, slice(0, MODES)), f)
                else:
                    tiles = [collect(k, slice(MODES, MODES + 8)) for k in range(7)]
                    split_into(jnp.concatenate(tiles, axis=0), f)
            multiply(p_ref, FACES, group, 1)

        def pair(j):
            def read(f):
                low = y_ref[1, j * FACE_PAD : (j + 1) * FACE_PAD, cols(f)]
                high = y_ref[1, (j + 1) * FACE_PAD : (j + 2) * FACE_PAD, cols(f)]
                return jnp.where(lane < E // 2, low, high)

            return by_field(read)

        g_ref[...] += gather([pair(0), pair(2)], ohr_ref)
        for i in range(4):
            turn = turn_ref[i : i + 1, :]
            for_one, for_two = turn == 1, turn == 2
            totals = [x_ref[i * FACE_PAD : (i + 1) * FACE_PAD, cols(g)] for g in range(FIELDS)]
            for f in range(FIELDS):
                raw = g_ref[f * FACE_PAD : (f + 1) * FACE_PAD, cols(i)]
                v = [raw[c * 8 : (c + 1) * 8] for c in range(3)]
                y = jnp.concatenate(
                    [
                        jnp.where(
                            for_one, v[(c + 1) % 3], jnp.where(for_two, v[(c + 2) % 3], v[c])
                        )
                        for c in range(3)
                    ],
                    axis=0,
                )
                for g in range(FIELDS):
                    totals[g] = totals[g] + minus_ref[f, g, i : i + 1, :] * y
            for g in range(FIELDS):
                x_ref[i * FACE_PAD : (i + 1) * FACE_PAD, cols(g)] = totals[g]

    def lifted(group):
        for g in group:
            high, low = high_low(x_ref[:, cols(g)])
            r_ref[0:FACES, cols(g)] = high.astype(BF)
            r_ref[FACES : 2 * FACES, cols(g)] = low.astype(BF)
        both = dot(l_ref[...], r_ref[:, cols(group[0], len(group))])
        return [
            both[0:MODES, cols(n)] + both[MODES : 2 * MODES, cols(n)] for n in range(len(group))
        ]

    first_stack()
    copies = exchange(0)
    for n in (7, 8, 9, 10, 5, 6, 2, 3, 11):
        loads[n].wait()
    small = cluster_ref[...] == 0
    other_operators(small)
    for f in range(FIELDS):
        base_ref[f] = sol_ref[f]
    pack_star()
    local_part()
    remote_part(0, copies)
    for group in GROUPS:
        update = lifted(group)
        for n, g in enumerate(group):
            base_ref[g] -= update[n]
    second_stack()
    copies = exchange(1)
    local_part()
    remote_part(1, copies)
    for group in GROUPS:
        update = lifted(group)
        for n, g in enumerate(group):
            out_ref[g] = base_ref[g] - update[n]


def on_device(
    n_dom,
    n_near,
    solution,
    star_matrices,
    flux_plus,
    flux_minus,
    stiffness,
    face_lift,
    face_project,
    cluster,
    neighbour_part,
    neighbour_slot,
    neighbour_face,
    orientation,
    halo_send,
):
    operands = (
        jnp.transpose(solution, (1, 0, 2)),
        jnp.transpose(star_matrices, (1, 2, 0, 3)),
        jnp.transpose(flux_plus, (1, 2, 0, 3)),
        jnp.transpose(flux_minus, (1, 2, 0, 3)),
        stiffness,
        jnp.transpose(face_lift, (2, 0, 1)),
        jnp.transpose(face_project, (1, 0, 2)),
        cluster.reshape(1, E),
        neighbour_part,
        neighbour_slot,
        neighbour_face,
        orientation,
        halo_send,
    )
    field_block = pltpu.VMEM((FIELDS, MODES, E), F32)
    step = pl.pallas_call(
        functools.partial(kernel, n_dom, n_near),
        out_shape=pltpu.VMEM((FIELDS, MODES, E), F32),
        in_specs=[pl.BlockSpec(memory_space=pltpu.HBM)] * 13,
        out_specs=pl.BlockSpec(memory_space=pltpu.VMEM),
        scratch_shapes=[pltpu.VMEM(value.shape, value.dtype) for value in operands]
        + [
            pltpu.VMEM((3 * KPAD, COLS), BF),
            pltpu.VMEM((2, FACES + 3 * MODES, COLS), F32),
            field_block,
            field_block,
            field_block,
            pltpu.VMEM((FACES, COLS), F32),
            pltpu.VMEM((FIELDS * FACE_PAD, 4 * E), F32),
            pltpu.VMEM((3 * MODES, 3 * KPAD), BF),
            pltpu.VMEM((FACES + 3 * MODES, 3 * KPAD), BF),
            pltpu.VMEM((FACES, 3 * KPAD), BF),
            pltpu.VMEM((2 * MODES, 2 * FACES), BF),
            pltpu.VMEM((4 * E, 4 * E), BF),
            pltpu.VMEM((16 * HALO, 4 * E), BF),
            pltpu.VMEM((2 * E, 4 * E), BF),
            pltpu.VMEM((2, 4, KPAD, E), F32),
            pltpu.VMEM((2, 4, KPAD, E), F32),
            pltpu.SemaphoreType.DMA((2, 4)),
            pltpu.SemaphoreType.DMA((2, 4)),
            pltpu.SemaphoreType.DMA((13,)),
            pltpu.VMEM((FIELDS, FIELDS, 3, 8, E), F32),
            pltpu.VMEM((len(PAIRS), FIELDS, 3, 8, E), F32),
            pltpu.VMEM((2 * E, E), BF),
            pltpu.VMEM((2 * E, 2 * E), BF),
            pltpu.VMEM((len(PAIRS), MODES, E), F32),
        ],
        compiler_params=pltpu.CompilerParams(
            collective_id=0, has_side_effects=True, vmem_limit_bytes=60 * 2**20
        ),
        name="cluster_step",
    )
    out = step(*operands)
    return jnp.transpose(out, (1, 0, 2))


def solution(mesh):
    both = ("dom", "near")
    in_specs = (
        P(None, None, both),
        P(None, None, None, both),
        P(None, None, None, both),
        P(None, None, None, both),
        P(),
        P(),
        P(),
        P(both),
        P(None, both),
        P(None, both),
        P(None, both),
        P(None, both),
        P(None, both),
    )
    return jax.shard_map(
        functools.partial(on_device, mesh.shape["dom"], mesh.shape["near"]),
        mesh=mesh,
        in_specs=in_specs,
        out_specs=P(None, None, both),
        check_vma=False,
    )
```

```python
import functools
import math

import jax
import jax.numpy as jnp
from jax import lax
from jax.experimental import pallas as pl
from jax.experimental.pallas import tpu as pltpu
from jax.sharding import PartitionSpec as P

MESH = pl.DeviceIdType.MESH
MODES = 56
FIELDS = 9
FACE_MODES = 21
ORDER = 6
E = 128
HALO = 16
PACK = 64
PAIRS = ((0, 1), (2, 3), (4, 5), (6, 7), (8,))
PAIR_GROUPS = ((0, 1), (2, 3), (4,))
KPAD = 64
FACE_PAD = 24
FACES = 4 * FACE_PAD
COLS = FIELDS * E
GROUPS = ((0, 1), (2, 3), (4, 5), (6, 7), (8,))
BF = jnp.bfloat16
F32 = jnp.float32


def orbit_nodes():
    degree = ORDER - 1
    nodes = [(a, b, degree - a - b) for a in range(degree + 1) for b in range(degree + 1 - a)]
    number = {node: n for n, node in enumerate(nodes)}
    seen, orbits = set(), []
    for node in nodes:
        if node in seen:
            continue
        a, b, c = node
        orbit = [(a, b, c), (b, c, a), (c, a, b)]
        seen.update(orbit)
        orbits.append([number[member] for member in orbit])
    order = [-1] * FACE_PAD
    for o, orbit in enumerate(orbits):
        for c in range(3):
            order[c * 8 + o] = orbit[c]
    return order


ORDERED = orbit_nodes()


def weights(begin, end):
    return [
        (end ** (k + 1) - begin ** (k + 1)) / math.factorial(k + 1) for k in range(ORDER)
    ]


def dot(a, b):
    return jnp.dot(a, b, preferred_element_type=F32)


def iota(shape, dim):
    return lax.broadcasted_iota(jnp.int32, shape, dim)


def ones_where(condition):
    return jnp.where(condition, 1.0, 0.0).astype(F32)


def high_low(x):
    high = x.astype(BF).astype(F32)
    return high, x - high


def place(x, marks):
    high, rest = high_low(x)
    middle, low = high_low(rest)
    marks = marks.astype(BF)
    return dot(high.astype(BF), marks) + dot(middle.astype(BF), marks) + dot(low.astype(BF), marks)


def place_left(marks, x):
    high, rest = high_low(x)
    middle, low = high_low(rest)
    marks = marks.astype(BF)
    return dot(marks, high.astype(BF)) + dot(marks, middle.astype(BF)) + dot(marks, low.astype(BF))


def threefold(matrix):
    high, low = high_low(matrix)
    row, col = iota((MODES, 3 * KPAD), 0), iota((MODES, 3 * KPAD), 1)
    twice = ones_where((col == row) | (col == row + KPAD)).astype(BF)
    last = ones_where(col == row + 2 * KPAD).astype(BF)
    return (dot(high.astype(BF), twice) + dot(low.astype(BF), last)).astype(BF)


def kernel(
    n_dom,
    n_near,
    *refs,
):
    sources, out_ref, held = refs[:13], refs[13], refs[14:27]
    (
        sol_ref,
        star_ref,
        plus_ref,
        minus_ref,
        stiff_ref,
        lift_ref,
        proj_ref,
        cluster_ref,
        part_ref,
        slot_ref,
        nface_ref,
        turn_ref,
        halo_ref,
    ) = held
    (
        y_ref,
        first_ref,
        second_ref,
        base_ref,
        x_ref,
        g_ref,
        a_ref,
        b_ref,
        p_ref,
        l_ref,
        ohl_ref,
        ohr_ref,
        ohs_ref,
        send_buf,
        recv_buf,
        send_sem,
        recv_sem,
        load_sem,
        star8_ref,
        packed_star_ref,
        compact_ref,
        widen_ref,
        j_ref,
    ) = refs[27:]
    loads = [
        pltpu.make_async_copy(source, target, load_sem.at[n])
        for n, (source, target) in enumerate(zip(sources, held))
    ]
    for n in (4, 0, 1, 12, 7, 8, 9, 10, 5, 6, 2, 3, 11):
        loads[n].start()
    dom, near = lax.axis_index("dom"), lax.axis_index("near")
    targets = (
        (dom, lax.rem(near + 1, n_near)),
        (dom, lax.rem(near + n_near - 1, n_near)),
        (lax.rem(dom + 1, n_dom), near),
        (lax.rem(dom + n_dom - 1, n_dom), near),
    )
    barrier = pltpu.get_barrier_semaphore()
    for target in targets:
        pl.semaphore_signal(barrier, inc=1, device_id=target, device_id_type=MESH)

    def cols(f, count=1):
        return slice(f * E, (f + count) * E)

    loads[4].wait()
    stiff = jnp.concatenate([stiff_ref[d] for d in range(3)], axis=0)
    a_ref[...] = threefold(stiff)

    held_parts = {}

    def split_into(t, f):
        high, low = high_low(t)
        zero = jnp.zeros((KPAD - MODES, E), F32)
        high = jnp.concatenate([high, zero], axis=0).astype(BF)
        low = jnp.concatenate([low, zero], axis=0).astype(BF)
        held_parts[f] = jnp.concatenate([high, low, high], axis=0)

    def multiply(matrix, rows, group, slot):
        columns = jnp.concatenate([held_parts[f] for f in group], axis=1)
        y_ref[slot, 0:rows, cols(group[0], len(group))] = dot(matrix[...], columns)

    def spread_mul(tile, y):
        return (tile[None] * y.reshape(MODES // 8, 8, E)).reshape(MODES, E)

    def star(group, slot, row0=0):
        totals = [None] * len(group)
        for d in range(3):
            for f in range(FIELDS):
                y = y_ref[slot, row0 + d * MODES : row0 + (d + 1) * MODES, cols(f)]
                for n, g in enumerate(group):
                    term = spread_mul(star8_ref[f, g, d], y)
                    totals[n] = term if totals[n] is None else totals[n] + term
        return totals

    half, rest = weights(0.0, 0.5), weights(0.5, 1.0)

    loads[0].wait()
    for group in GROUPS:
        for f in group:
            u = sol_ref[f]
            split_into(u, f)
            first_ref[f] = half[0] * u
            second_ref[f] = rest[0] * u
        multiply(a_ref, 3 * MODES, group, 0)

    for n in (1, 12):
        loads[n].wait()
    for f in range(FIELDS):
        for g in range(FIELDS):
            for d in range(3):
                star8_ref[f, g, d] = jnp.broadcast_to(star_ref[f, g, d : d + 1, :], (8, E))
    spread = ones_where(iota((HALO, E), 0) == lax.rem(iota((HALO, E), 1), HALO)).astype(BF)
    sent = dot(halo_ref[...].astype(F32).astype(BF), spread)
    for r in range(4):
        ohs_ref[:, cols(r)] = ones_where(
            sent[r : r + 1, :] == iota((2 * E, E), 0).astype(F32)
        ).astype(BF) + ones_where(
            sent[r : r + 1, :] + float(E) == iota((2 * E, E), 0).astype(F32)
        ).astype(BF)

    lane = iota((1, E), 1)
    lane_group = lane // HALO

    def first_stack():
        for k in range(ORDER - 2):
            for group in GROUPS:
                for g, t in zip(group, star(group, k % 2)):
                    split_into(t, g)
                    first_ref[g] += half[k + 1] * t
                    second_ref[g] += rest[k + 1] * t
                multiply(a_ref, 3 * MODES, group, (k + 1) % 2)
        for group in GROUPS:
            for g, t in zip(group, star(group, 0)):
                first_ref[g] += half[5] * t
                second_ref[g] += rest[5] * t

    def other_operators(small):
        backward = jnp.concatenate([stiff_ref[d].T for d in range(3)], axis=0)
        node, entry = iota((FACE_PAD, FACE_MODES), 1), iota((FACE_PAD, FACE_MODES), 0)
        chosen = entry < 0
        for spot, number in enumerate(ORDERED):
            if number >= 0:
                chosen = chosen | ((entry == spot) & (node == number))
        chosen = ones_where(chosen)
        project = jnp.concatenate([place_left(chosen, proj_ref[:, j, :]) for j in range(4)], axis=0)
        lifts = jnp.concatenate([place_left(chosen, lift_ref[:, j, :]) for j in range(4)], axis=0)
        b_ref[...] = threefold(jnp.concatenate([project, backward], axis=0))
        p_ref[...] = threefold(project)
        lift_high, lift_low = high_low(lifts.T)
        row, col = iota((FACES, 2 * FACES), 0), iota((FACES, 2 * FACES), 1)
        twice = ones_where((col == row) | (col == row + FACES)).astype(BF)
        once = ones_where(col == row).astype(BF)
        l_ref[...] = jnp.concatenate(
            [dot(lift_high.astype(BF), twice), dot(lift_low.astype(BF), once)], axis=0
        ).astype(BF)

        part, slot_of = part_ref[...], slot_ref[...]
        face_of = nface_ref[...]
        local_key = jnp.where(part == 0, face_of * E + slot_of, -1)
        remote_key = jnp.where(part > 0, face_of * (4 * HALO) + (part - 1) * HALO + slot_of, -1)
        for i in range(4):
            ohl_ref[:, cols(i)] = ones_where(local_key[i : i + 1, :] == iota((4 * E, E), 0)).astype(BF)
            ohr_ref[:, cols(i)] = ones_where(
                remote_key[i : i + 1, :] == iota((16 * HALO, E), 0)
            ).astype(BF)
        before = ones_where(iota((E, E), 0) < iota((E, E), 1)).astype(BF)
        small_row = ones_where(small)
        rank_row = dot(jnp.broadcast_to(small_row, (8, E)).astype(BF), before)[0:1]
        rank_row = jnp.where(small, rank_row, -1.0)
        square = iota((E, E), 0) == iota((E, E), 1)
        rank_col = jnp.sum(jnp.where(square, rank_row, 0.0), axis=1, keepdims=True)
        place_of = lax.rem(iota((E, E), 1), PACK).astype(F32)
        compact = ones_where(rank_col == place_of).astype(BF)
        compact_ref[0:E] = compact
        compact_ref[E : 2 * E] = compact
        source = iota((E, E), 0)
        for h in range(2):
            wide = ones_where(rank_row == (source - h * PACK).astype(F32)).astype(BF)
            widen_ref[0:E, cols(h)] = wide
            widen_ref[E : 2 * E, cols(h)] = wide

    lower = lane < PACK

    def sides(block):
        high, low = high_low(block)
        return jnp.concatenate([high.astype(BF), low.astype(BF)], axis=1)

    def pack_star():
        rows = FIELDS * 3 * 8
        for p, pair in enumerate(PAIRS):
            taken = [
                dot(sides(star8_ref[f].reshape(rows, E)), compact_ref[...]) for f in pair
            ]
            both = jnp.where(lower, taken[0], taken[1] if len(pair) == 2 else 0.0)
            packed_star_ref[p] = both.reshape(FIELDS, 3, 8, E)

    def packed_star(pairs, slot):
        fields = [g for p in pairs for g in PAIRS[p]]
        totals = dict.fromkeys(fields)
        for d in range(3):
            for q in range(len(PAIRS)):
                y = y_ref[slot, d * MODES : (d + 1) * MODES, cols(q)]
                for g in fields:
                    term = spread_mul(packed_star_ref[q, g, d], y)
                    totals[g] = term if totals[g] is None else totals[g] + term
        folded = []
        for p in pairs:
            one = totals[PAIRS[p][0]]
            if len(PAIRS[p]) == 2:
                two = totals[PAIRS[p][1]]
                folded.append(
                    jnp.where(lower, one, two) + pltpu.roll(jnp.where(lower, two, one), PACK, 1)
                )
            else:
                folded.append(jnp.where(lower, one + pltpu.roll(one, PACK, 1), 0.0))
        return folded

    def second_stack():
        for group in PAIR_GROUPS:
            for p in group:
                taken = [dot(sides(base_ref[f]), compact_ref[...]) for f in PAIRS[p]]
                u = jnp.where(lower, taken[0], taken[1] if len(taken) == 2 else 0.0)
                split_into(u, p)
                j_ref[p] = half[0] * u
            multiply(a_ref, 3 * MODES, group, 0)
        for k in range(ORDER - 2):
            for group in PAIR_GROUPS:
                for p, t in zip(group, packed_star(group, k % 2)):
                    split_into(t, p)
                    j_ref[p] += half[k + 1] * t
                multiply(a_ref, 3 * MODES, group, (k + 1) % 2)
        for group in PAIR_GROUPS:
            for p, t in zip(group, packed_star(group, 0)):
                wide = dot(sides(j_ref[p] + half[5] * t), widen_ref[...])
                for n, f in enumerate(PAIRS[p]):
                    first_ref[f] = jnp.where(small, wide[:, cols(n)], second_ref[f])

    def exchange(phase):
        copies = []
        highs, lows = [], []
        for f in range(FIELDS):
            high, low = high_low(first_ref[f])
            highs.append(high)
            lows.append(low)
        stacked = jnp.concatenate(
            [
                jnp.concatenate(highs, axis=0).astype(BF),
                jnp.concatenate(lows, axis=0).astype(BF),
            ],
            axis=1,
        )
        for pair in ((2, 3), (0, 1)):
            taken = dot(stacked, ohs_ref[:, cols(pair[0], 2)])
            for n, r in enumerate(pair):
                block = taken[:, cols(n)]
                packed = block[0:MODES]
                for f in range(1, 8):
                    packed = jnp.where(lane_group == f, block[f * MODES : (f + 1) * MODES], packed)
                tail = block[8 * MODES : 8 * MODES + 8]
                for k in range(1, 7):
                    start = 8 * MODES + 8 * k
                    tail = jnp.where(lane_group == k, block[start : start + 8], tail)
                send_buf[phase, r] = jnp.concatenate([packed, tail], axis=0)
            if phase == 0 and pair[0] == 2:
                pl.semaphore_wait(barrier, 4)
            for r in pair:
                copy = pltpu.make_async_remote_copy(
                    src_ref=send_buf.at[phase, r],
                    dst_ref=recv_buf.at[phase, r],
                    send_sem=send_sem.at[phase, r],
                    recv_sem=recv_sem.at[phase, r],
                    device_id=targets[r],
                    device_id_type=MESH,
                )
                copy.start()
                copies.append(copy)
        return copies

    def gather(blocks, marks):
        sides = []
        for block in blocks:
            high, low = high_low(block)
            sides.append(jnp.concatenate([high, low], axis=0).astype(BF))
        both = dot(jnp.concatenate(sides, axis=1), marks[...])
        rows = FIELDS * FACE_PAD
        return both[0:rows] + both[rows : 2 * rows]

    def by_field(read):
        return jnp.concatenate([read(f) for f in range(FIELDS)], axis=0)

    def local_part():
        for group in GROUPS:
            for f in group:
                split_into(first_ref[f], f)
            multiply(b_ref, FACES + 3 * MODES, group, 0)
        g_ref[...] = gather(
            [
                by_field(lambda f: y_ref[0, j * FACE_PAD : (j + 1) * FACE_PAD, cols(f)])
                for j in range(4)
            ],
            ohl_ref,
        )
        for i in range(4):
            totals = [None] * FIELDS
            for f in range(FIELDS):
                y = y_ref[0, i * FACE_PAD : (i + 1) * FACE_PAD, cols(f)]
                for g in range(FIELDS):
                    term = plus_ref[f, g, i : i + 1, :] * y
                    totals[g] = term if totals[g] is None else totals[g] + term
            for g in range(FIELDS):
                x_ref[i * FACE_PAD : (i + 1) * FACE_PAD, cols(g)] = totals[g]
        for group in GROUPS:
            for g, v in zip(group, star(group, 0, FACES)):
                base_ref[g] += v

    def remote_part(phase, copies):
        for copy in copies:
            copy.wait()
        rolled = []
        for r in range(4):
            block = recv_buf[phase, r]
            rolled.append(
                [block if c == 0 else pltpu.roll(block, c * HALO, 1) for c in range(8)]
            )

        def collect(at, rows):
            value = None
            for spot in range(8):
                r = spot % 4
                piece = rolled[r][(spot - at) % 8][rows]
                value = piece if value is None else jnp.where(lane_group == spot, piece, value)
            return value

        for group in GROUPS:
            for f in group:
                if f < 8:
                    split_into(collect(f, slice(0, MODES)), f)
                else:
                    tiles = [collect(k, slice(MODES, MODES + 8)) for k in range(7)]
                    split_into(jnp.concatenate(tiles, axis=0), f)
            multiply(p_ref, FACES, group, 1)

        def pair(j):
            def read(f):
                low = y_ref[1, j * FACE_PAD : (j + 1) * FACE_PAD, cols(f)]
                high = y_ref[1, (j + 1) * FACE_PAD : (j + 2) * FACE_PAD, cols(f)]
                return jnp.where(lane < E // 2, low, high)

            return by_field(read)

        g_ref[...] += gather([pair(0), pair(2)], ohr_ref)
        for i in range(4):
            turn = turn_ref[i : i + 1, :]
            for_one, for_two = turn == 1, turn == 2
            for f in range(FIELDS):
                raw = g_ref[f * FACE_PAD : (f + 1) * FACE_PAD, cols(i)]
                v = [raw[c * 8 : (c + 1) * 8] for c in range(3)]
                g_ref[f * FACE_PAD : (f + 1) * FACE_PAD, cols(i)] = jnp.concatenate(
                    [
                        jnp.where(
                            for_one, v[(c + 1) % 3], jnp.where(for_two, v[(c + 2) % 3], v[c])
                        )
                        for c in range(3)
                    ],
                    axis=0,
                )

    def outside(group):
        totals = [
            [x_ref[i * FACE_PAD : (i + 1) * FACE_PAD, cols(g)] for i in range(4)] for g in group
        ]
        for f in range(FIELDS):
            for i in range(4):
                y = g_ref[f * FACE_PAD : (f + 1) * FACE_PAD, cols(i)]
                for n, g in enumerate(group):
                    totals[n][i] = totals[n][i] + minus_ref[f, g, i : i + 1, :] * y
        return [jnp.concatenate(total, axis=0) for total in totals]

    def lifted(group):
        parts = []
        for g, flux in zip(group, outside(group)):
            high, low = high_low(flux)
            parts.append(jnp.concatenate([high.astype(BF), low.astype(BF)], axis=0))
        both = dot(l_ref[...], jnp.concatenate(parts, axis=1))
        return [
            both[0:MODES, cols(n)] + both[MODES : 2 * MODES, cols(n)] for n in range(len(group))
        ]

    first_stack()
    copies = exchange(0)
    for n in (7, 8, 9, 10, 5, 6, 2, 3, 11):
        loads[n].wait()
    small = cluster_ref[...] == 0
    other_operators(small)
    for f in range(FIELDS):
        base_ref[f] = sol_ref[f]
    pack_star()
    local_part()
    remote_part(0, copies)
    for group in GROUPS:
        update = lifted(group)
        for n, g in enumerate(group):
            base_ref[g] -= update[n]
    second_stack()
    copies = exchange(1)
    local_part()
    remote_part(1, copies)
    for group in GROUPS:
        update = lifted(group)
        for n, g in enumerate(group):
            out_ref[g] = base_ref[g] - update[n]


def on_device(
    n_dom,
    n_near,
    solution,
    star_matrices,
    flux_plus,
    flux_minus,
    stiffness,
    face_lift,
    face_project,
    cluster,
    neighbour_part,
    neighbour_slot,
    neighbour_face,
    orientation,
    halo_send,
):
    operands = (
        jnp.transpose(solution, (1, 0, 2)),
        jnp.transpose(star_matrices, (1, 2, 0, 3)),
        jnp.transpose(flux_plus, (1, 2, 0, 3)),
        jnp.transpose(flux_minus, (1, 2, 0, 3)),
        stiffness,
        jnp.transpose(face_lift, (2, 0, 1)),
        jnp.transpose(face_project, (1, 0, 2)),
        cluster.reshape(1, E),
        neighbour_part,
        neighbour_slot,
        neighbour_face,
        orientation,
        halo_send,
    )
    field_block = pltpu.VMEM((FIELDS, MODES, E), F32)
    step = pl.pallas_call(
        functools.partial(kernel, n_dom, n_near),
        out_shape=pltpu.VMEM((FIELDS, MODES, E), F32),
        in_specs=[pl.BlockSpec(memory_space=pltpu.HBM)] * 13,
        out_specs=pl.BlockSpec(memory_space=pltpu.VMEM),
        scratch_shapes=[pltpu.VMEM(value.shape, value.dtype) for value in operands]
        + [
            pltpu.VMEM((2, FACES + 3 * MODES, COLS), F32),
            field_block,
            field_block,
            field_block,
            pltpu.VMEM((FACES, COLS), F32),
            pltpu.VMEM((FIELDS * FACE_PAD, 4 * E), F32),
            pltpu.VMEM((3 * MODES, 3 * KPAD), BF),
            pltpu.VMEM((FACES + 3 * MODES, 3 * KPAD), BF),
            pltpu.VMEM((FACES, 3 * KPAD), BF),
            pltpu.VMEM((2 * MODES, 2 * FACES), BF),
            pltpu.VMEM((4 * E, 4 * E), BF),
            pltpu.VMEM((16 * HALO, 4 * E), BF),
            pltpu.VMEM((2 * E, 4 * E), BF),
            pltpu.VMEM((2, 4, KPAD, E), F32),
            pltpu.VMEM((2, 4, KPAD, E), F32),
            pltpu.SemaphoreType.DMA((2, 4)),
            pltpu.SemaphoreType.DMA((2, 4)),
            pltpu.SemaphoreType.DMA((13,)),
            pltpu.VMEM((FIELDS, FIELDS, 3, 8, E), F32),
            pltpu.VMEM((len(PAIRS), FIELDS, 3, 8, E), F32),
            pltpu.VMEM((2 * E, E), BF),
            pltpu.VMEM((2 * E, 2 * E), BF),
            pltpu.VMEM((len(PAIRS), MODES, E), F32),
        ],
        compiler_params=pltpu.CompilerParams(
            collective_id=0, has_side_effects=True, vmem_limit_bytes=60 * 2**20
        ),
        name="cluster_step",
    )
    out = step(*operands)
    return jnp.transpose(out, (1, 0, 2))


def solution(mesh):
    both = ("dom", "near")
    in_specs = (
        P(None, None, both),
        P(None, None, None, both),
        P(None, None, None, both),
        P(None, None, None, both),
        P(),
        P(),
        P(),
        P(both),
        P(None, both),
        P(None, both),
        P(None, both),
        P(None, both),
        P(None, both),
    )
    return jax.shard_map(
        functools.partial(on_device, mesh.shape["dom"], mesh.shape["near"]),
        mesh=mesh,
        in_specs=in_specs,
        out_specs=P(None, None, both),
        check_vma=False,
    )
```

```python
import functools
import math

import jax
import jax.numpy as jnp
from jax import lax
from jax.experimental import pallas as pl
from jax.experimental.pallas import tpu as pltpu
from jax.sharding import PartitionSpec as P

MESH = pl.DeviceIdType.MESH
MODES = 56
FIELDS = 9
FACE_MODES = 21
ORDER = 6
E = 128
HALO = 16
PACK = 64
PAIRS = ((0, 1), (2, 3), (4, 5), (6, 7), (8,))
PAIR_GROUPS = ((0, 1), (2, 3), (4,))
KPAD = 64
FACE_PAD = 24
FACES = 4 * FACE_PAD
COLS = FIELDS * E
GROUPS = ((0, 1), (2, 3), (4, 5), (6, 7), (8,))
BF = jnp.bfloat16
F32 = jnp.float32


def orbit_nodes():
    degree = ORDER - 1
    nodes = [(a, b, degree - a - b) for a in range(degree + 1) for b in range(degree + 1 - a)]
    number = {node: n for n, node in enumerate(nodes)}
    seen, orbits = set(), []
    for node in nodes:
        if node in seen:
            continue
        a, b, c = node
        orbit = [(a, b, c), (b, c, a), (c, a, b)]
        seen.update(orbit)
        orbits.append([number[member] for member in orbit])
    order = [-1] * FACE_PAD
    for o, orbit in enumerate(orbits):
        for c in range(3):
            order[c * 8 + o] = orbit[c]
    return order


ORDERED = orbit_nodes()


def weights(begin, end):
    return [
        (end ** (k + 1) - begin ** (k + 1)) / math.factorial(k + 1) for k in range(ORDER)
    ]


def dot(a, b):
    return jnp.dot(a, b, preferred_element_type=F32)


def iota(shape, dim):
    return lax.broadcasted_iota(jnp.int32, shape, dim)


def ones_where(condition):
    return jnp.where(condition, 1.0, 0.0).astype(F32)


def high_low(x):
    high = x.astype(BF).astype(F32)
    return high, x - high


def place(x, marks):
    high, rest = high_low(x)
    middle, low = high_low(rest)
    marks = marks.astype(BF)
    return dot(high.astype(BF), marks) + dot(middle.astype(BF), marks) + dot(low.astype(BF), marks)


def place_left(marks, x):
    high, rest = high_low(x)
    middle, low = high_low(rest)
    marks = marks.astype(BF)
    return dot(marks, high.astype(BF)) + dot(marks, middle.astype(BF)) + dot(marks, low.astype(BF))


def threefold(matrix):
    high, low = high_low(matrix)
    row, col = iota((MODES, 3 * KPAD), 0), iota((MODES, 3 * KPAD), 1)
    twice = ones_where((col == row) | (col == row + KPAD)).astype(BF)
    last = ones_where(col == row + 2 * KPAD).astype(BF)
    return (dot(high.astype(BF), twice) + dot(low.astype(BF), last)).astype(BF)


def kernel(
    n_dom,
    n_near,
    *refs,
):
    sources, out_ref, held = refs[:13], refs[13], refs[14:27]
    (
        sol_ref,
        star_ref,
        plus_ref,
        minus_ref,
        stiff_ref,
        lift_ref,
        proj_ref,
        cluster_ref,
        part_ref,
        slot_ref,
        nface_ref,
        turn_ref,
        halo_ref,
    ) = held
    (
        y_ref,
        first_ref,
        second_ref,
        base_ref,
        x_ref,
        g_ref,
        a_ref,
        b_ref,
        p_ref,
        l_ref,
        ohl_ref,
        ohr_ref,
        ohs_ref,
        send_buf,
        recv_buf,
        send_sem,
        recv_sem,
        load_sem,
        star8_ref,
        packed_star_ref,
        compact_ref,
        widen_ref,
        j_ref,
        pick_ref,
        slot_ints,
        minus8_ref,
    ) = refs[27:]
    loads = [
        pltpu.make_async_copy(source, target, load_sem.at[n])
        for n, (source, target) in enumerate(zip(sources, held))
    ]
    for n in (4, 0, 1, 12, 7, 8, 9, 10, 5, 6, 2, 3, 11):
        loads[n].start()
    dom, near = lax.axis_index("dom"), lax.axis_index("near")
    targets = (
        (dom, lax.rem(near + 1, n_near)),
        (dom, lax.rem(near + n_near - 1, n_near)),
        (lax.rem(dom + 1, n_dom), near),
        (lax.rem(dom + n_dom - 1, n_dom), near),
    )
    barrier = pltpu.get_barrier_semaphore()
    for target in targets:
        pl.semaphore_signal(barrier, inc=1, device_id=target, device_id_type=MESH)

    def cols(f, count=1):
        return slice(f * E, (f + count) * E)

    loads[4].wait()
    stiff = jnp.concatenate([stiff_ref[d] for d in range(3)], axis=0)
    a_ref[...] = threefold(stiff)

    held_parts = {}

    def split_into(t, f):
        high, low = high_low(t)
        zero = jnp.zeros((KPAD - MODES, E), F32)
        high = jnp.concatenate([high, zero], axis=0).astype(BF)
        low = jnp.concatenate([low, zero], axis=0).astype(BF)
        held_parts[f] = jnp.concatenate([high, low, high], axis=0)

    def multiply(matrix, rows, group, slot):
        columns = jnp.concatenate([held_parts[f] for f in group], axis=1)
        y_ref[slot, 0:rows, cols(group[0], len(group))] = dot(matrix[...], columns)

    def spread_mul(tile, y):
        return (tile[None] * y.reshape(MODES // 8, 8, E)).reshape(MODES, E)

    def star(group, slot, row0=0):
        totals = [None] * len(group)
        for d in range(3):
            for f in range(FIELDS):
                y = y_ref[slot, row0 + d * MODES : row0 + (d + 1) * MODES, cols(f)]
                for n, g in enumerate(group):
                    term = spread_mul(star8_ref[f, g, d], y)
                    totals[n] = term if totals[n] is None else totals[n] + term
        return totals

    half, rest = weights(0.0, 0.5), weights(0.5, 1.0)

    loads[0].wait()
    for group in GROUPS:
        for f in group:
            u = sol_ref[f]
            split_into(u, f)
            first_ref[f] = half[0] * u
            second_ref[f] = rest[0] * u
        multiply(a_ref, 3 * MODES, group, 0)

    for n in (1, 12):
        loads[n].wait()
    for f in range(FIELDS):
        for g in range(FIELDS):
            for d in range(3):
                star8_ref[f, g, d] = jnp.broadcast_to(star_ref[f, g, d : d + 1, :], (8, E))
    spread = ones_where(iota((HALO, E), 0) == lax.rem(iota((HALO, E), 1), HALO)).astype(BF)
    sent = dot(halo_ref[...].astype(F32).astype(BF), spread)
    for r in range(4):
        ohs_ref[:, cols(r)] = ones_where(
            sent[r : r + 1, :] == iota((2 * E, E), 0).astype(F32)
        ).astype(BF) + ones_where(
            sent[r : r + 1, :] + float(E) == iota((2 * E, E), 0).astype(F32)
        ).astype(BF)

    lane = iota((1, E), 1)
    lane_group = lane // HALO

    def first_stack():
        for k in range(ORDER - 2):
            for group in GROUPS:
                for g, t in zip(group, star(group, k % 2)):
                    split_into(t, g)
                    first_ref[g] += half[k + 1] * t
                    second_ref[g] += rest[k + 1] * t
                multiply(a_ref, 3 * MODES, group, (k + 1) % 2)
        for group in GROUPS:
            for g, t in zip(group, star(group, 0)):
                first_ref[g] += half[5] * t
                second_ref[g] += rest[5] * t

    def other_operators(small):
        backward = jnp.concatenate([stiff_ref[d].T for d in range(3)], axis=0)
        node, entry = iota((FACE_PAD, FACE_MODES), 1), iota((FACE_PAD, FACE_MODES), 0)
        chosen = entry < 0
        for spot, number in enumerate(ORDERED):
            if number >= 0:
                chosen = chosen | ((entry == spot) & (node == number))
        chosen = ones_where(chosen)
        project = jnp.concatenate([place_left(chosen, proj_ref[:, j, :]) for j in range(4)], axis=0)
        lifts = jnp.concatenate([place_left(chosen, lift_ref[:, j, :]) for j in range(4)], axis=0)
        b_ref[...] = threefold(jnp.concatenate([project, backward], axis=0))
        p_ref[...] = threefold(project)
        lift_high, lift_low = high_low(lifts.T)
        row, col = iota((FACES, 2 * FACES), 0), iota((FACES, 2 * FACES), 1)
        twice = ones_where((col == row) | (col == row + FACES)).astype(BF)
        once = ones_where(col == row).astype(BF)
        l_ref[...] = jnp.concatenate(
            [dot(lift_high.astype(BF), twice), dot(lift_low.astype(BF), once)], axis=0
        ).astype(BF)

        part, slot_of = part_ref[...], slot_ref[...]
        face_of = nface_ref[...]
        local_key = jnp.where(part == 0, face_of * E + slot_of, -1)
        slot_key = jnp.where(part > 0, (part - 1) * HALO + slot_of, -1).astype(F32)
        diagonal = iota((E, E), 0) == iota((E, E), 1)
        slot_lane = lax.rem(iota((E, E), 1), PACK).astype(F32)
        for i in range(4):
            ohl_ref[:, cols(i)] = ones_where(local_key[i : i + 1, :] == iota((4 * E, E), 0)).astype(BF)
            key = slot_key[i : i + 1, :]
            scatter = ones_where(key == iota((E, E), 0).astype(F32)).astype(BF)
            ohr_ref[0:E, cols(i)] = scatter
            ohr_ref[E : 2 * E, cols(i)] = scatter
            key_col = jnp.sum(jnp.where(diagonal, key, 0.0), axis=1, keepdims=True)
            pick_ref[i * E : (i + 1) * E, :] = ones_where(key_col == slot_lane).astype(BF)
        for n, table in enumerate((face_of, turn_ref[...])):
            line = jnp.concatenate([table[i : i + 1, :] for i in range(4)], axis=1).astype(F32)
            slot_ints[n] = dot(jnp.broadcast_to(line, (8, 4 * E)).astype(BF), pick_ref[...])
        for f in range(FIELDS):
            line = jnp.concatenate(
                [
                    jnp.concatenate(
                        [
                            jnp.broadcast_to(minus_ref[f, g, i : i + 1, :], (8, E))
                            for g in range(FIELDS)
                        ],
                        axis=0,
                    )
                    for i in range(4)
                ],
                axis=1,
            )
            high, low = high_low(line)
            both = dot(high.astype(BF), pick_ref[...]) + dot(low.astype(BF), pick_ref[...])
            minus8_ref[f] = both.reshape(FIELDS, 8, E)
        before = ones_where(iota((E, E), 0) < iota((E, E), 1)).astype(BF)
        small_row = ones_where(small)
        rank_row = dot(jnp.broadcast_to(small_row, (8, E)).astype(BF), before)[0:1]
        rank_row = jnp.where(small, rank_row, -1.0)
        square = iota((E, E), 0) == iota((E, E), 1)
        rank_col = jnp.sum(jnp.where(square, rank_row, 0.0), axis=1, keepdims=True)
        place_of = lax.rem(iota((E, E), 1), PACK).astype(F32)
        compact = ones_where(rank_col == place_of).astype(BF)
        compact_ref[0:E] = compact
        compact_ref[E : 2 * E] = compact
        source = iota((E, E), 0)
        for h in range(2):
            wide = ones_where(rank_row == (source - h * PACK).astype(F32)).astype(BF)
            widen_ref[0:E, cols(h)] = wide
            widen_ref[E : 2 * E, cols(h)] = wide

    lower = lane < PACK

    def sides(block):
        high, low = high_low(block)
        return jnp.concatenate([high.astype(BF), low.astype(BF)], axis=1)

    def pack_star():
        rows = FIELDS * 3 * 8
        for p, pair in enumerate(PAIRS):
            taken = [
                dot(sides(star8_ref[f].reshape(rows, E)), compact_ref[...]) for f in pair
            ]
            both = jnp.where(lower, taken[0], taken[1] if len(pair) == 2 else 0.0)
            packed_star_ref[p] = both.reshape(FIELDS, 3, 8, E)

    def packed_star(pairs, slot):
        fields = [g for p in pairs for g in PAIRS[p]]
        totals = dict.fromkeys(fields)
        for d in range(3):
            for q in range(len(PAIRS)):
                y = y_ref[slot, d * MODES : (d + 1) * MODES, cols(q)]
                for g in fields:
                    term = spread_mul(packed_star_ref[q, g, d], y)
                    totals[g] = term if totals[g] is None else totals[g] + term
        folded = []
        for p in pairs:
            one = totals[PAIRS[p][0]]
            if len(PAIRS[p]) == 2:
                two = totals[PAIRS[p][1]]
                folded.append(
                    jnp.where(lower, one, two) + pltpu.roll(jnp.where(lower, two, one), PACK, 1)
                )
            else:
                folded.append(jnp.where(lower, one + pltpu.roll(one, PACK, 1), 0.0))
        return folded

    def second_stack():
        for group in PAIR_GROUPS:
            for p in group:
                taken = dot(
                    sides(jnp.concatenate([base_ref[f] for f in PAIRS[p]], axis=0)),
                    compact_ref[...],
                )
                taken = [taken[n * MODES : (n + 1) * MODES] for n in range(len(PAIRS[p]))]
                u = jnp.where(lower, taken[0], taken[1] if len(taken) == 2 else 0.0)
                split_into(u, p)
                j_ref[p] = half[0] * u
            multiply(a_ref, 3 * MODES, group, 0)
        for k in range(ORDER - 2):
            for group in PAIR_GROUPS:
                for p, t in zip(group, packed_star(group, k % 2)):
                    split_into(t, p)
                    j_ref[p] += half[k + 1] * t
                multiply(a_ref, 3 * MODES, group, (k + 1) % 2)
        for group in PAIR_GROUPS:
            for p, t in zip(group, packed_star(group, 0)):
                wide = dot(sides(j_ref[p] + half[5] * t), widen_ref[...])
                for n, f in enumerate(PAIRS[p]):
                    first_ref[f] = jnp.where(small, wide[:, cols(n)], second_ref[f])

    def exchange(phase):
        copies = []
        highs, lows = [], []
        for f in range(FIELDS):
            high, low = high_low(first_ref[f])
            highs.append(high)
            lows.append(low)
        stacked = jnp.concatenate(
            [
                jnp.concatenate(highs, axis=0).astype(BF),
                jnp.concatenate(lows, axis=0).astype(BF),
            ],
            axis=1,
        )
        for pair in ((2, 3), (0, 1)):
            taken = dot(stacked, ohs_ref[:, cols(pair[0], 2)])
            for n, r in enumerate(pair):
                block = taken[:, cols(n)]
                packed = block[0:MODES]
                for f in range(1, 8):
                    packed = jnp.where(lane_group == f, block[f * MODES : (f + 1) * MODES], packed)
                tail = block[8 * MODES : 8 * MODES + 8]
                for k in range(1, 7):
                    start = 8 * MODES + 8 * k
                    tail = jnp.where(lane_group == k, block[start : start + 8], tail)
                send_buf[phase, r] = jnp.concatenate([packed, tail], axis=0)
            if phase == 0 and pair[0] == 2:
                pl.semaphore_wait(barrier, 4)
            for r in pair:
                copy = pltpu.make_async_remote_copy(
                    src_ref=send_buf.at[phase, r],
                    dst_ref=recv_buf.at[phase, r],
                    send_sem=send_sem.at[phase, r],
                    recv_sem=recv_sem.at[phase, r],
                    device_id=targets[r],
                    device_id_type=MESH,
                )
                copy.start()
                copies.append(copy)
        return copies

    def gather(blocks, marks):
        tall = []
        for block in blocks:
            high, low = high_low(block)
            tall.append(jnp.concatenate([high, low], axis=0).astype(BF))
        both = dot(jnp.concatenate(tall, axis=1), marks[...])
        rows = FIELDS * FACE_PAD
        return both[0:rows] + both[rows : 2 * rows]

    def by_field(read):
        return jnp.concatenate([read(f) for f in range(FIELDS)], axis=0)

    def rotated(raw, for_one, for_two):
        v = [raw[c * 8 : (c + 1) * 8] for c in range(3)]
        return jnp.concatenate(
            [
                jnp.where(for_one, v[(c + 1) % 3], jnp.where(for_two, v[(c + 2) % 3], v[c]))
                for c in range(3)
            ],
            axis=0,
        )

    def local_part():
        for group in GROUPS:
            for f in group:
                split_into(first_ref[f], f)
            multiply(b_ref, FACES + 3 * MODES, group, 0)
        g_ref[...] = gather(
            [
                by_field(lambda f: y_ref[0, j * FACE_PAD : (j + 1) * FACE_PAD, cols(f)])
                for j in range(4)
            ],
            ohl_ref,
        )
        for i in range(4):
            totals = [None] * FIELDS
            turn = turn_ref[i : i + 1, :]
            for f in range(FIELDS):
                y = y_ref[0, i * FACE_PAD : (i + 1) * FACE_PAD, cols(f)]
                z = rotated(g_ref[f * FACE_PAD : (f + 1) * FACE_PAD, cols(i)], turn == 1, turn == 2)
                for g in range(FIELDS):
                    term = plus_ref[f, g, i : i + 1, :] * y + minus_ref[f, g, i : i + 1, :] * z
                    totals[g] = term if totals[g] is None else totals[g] + term
            for g in range(FIELDS):
                x_ref[i * FACE_PAD : (i + 1) * FACE_PAD, cols(g)] = totals[g]
        for group in GROUPS:
            for g, v in zip(group, star(group, 0, FACES)):
                base_ref[g] += v

    def remote_part(phase, copies):
        for copy in copies:
            copy.wait()
        rolled = []
        for r in range(4):
            block = recv_buf[phase, r]
            rolled.append(
                [block if c == 0 else pltpu.roll(block, c * HALO, 1) for c in range(8)]
            )

        def collect(at, rows):
            value = None
            for spot in range(8):
                r = spot % 4
                piece = rolled[r][(spot - at) % 8][rows]
                value = piece if value is None else jnp.where(lane_group == spot, piece, value)
            return value

        for group in GROUPS:
            for f in group:
                if f < 8:
                    split_into(collect(f, slice(0, MODES)), f)
                else:
                    tiles = [collect(k, slice(MODES, MODES + 8)) for k in range(7)]
                    split_into(jnp.concatenate(tiles, axis=0), f)
            multiply(p_ref, FACES, group, 1)

        face, turn = slot_ints[0, 0:1, :], slot_ints[1, 0:1, :]
        totals = [None] * FIELDS
        for f in range(FIELDS):
            t = [y_ref[1, j * FACE_PAD : (j + 1) * FACE_PAD, cols(f)] for j in range(4)]
            own = jnp.where(
                face == 0.0, t[0], jnp.where(face == 1.0, t[1], jnp.where(face == 2.0, t[2], t[3]))
            )
            y = rotated(own, turn == 1.0, turn == 2.0)
            for g in range(FIELDS):
                term = (minus8_ref[f, g][None] * y.reshape(3, 8, E)).reshape(FACE_PAD, E)
                totals[g] = term if totals[g] is None else totals[g] + term
        g_ref[...] = dot(sides(jnp.concatenate(totals, axis=0)), ohr_ref[...])

    def outside(group):
        return [
            x_ref[:, cols(g)]
            + jnp.concatenate(
                [g_ref[g * FACE_PAD : (g + 1) * FACE_PAD, cols(i)] for i in range(4)], axis=0
            )
            for g in group
        ]

    def lifted(group):
        parts = []
        for g, flux in zip(group, outside(group)):
            high, low = high_low(flux)
            parts.append(jnp.concatenate([high.astype(BF), low.astype(BF)], axis=0))
        both = dot(l_ref[...], jnp.concatenate(parts, axis=1))
        return [
            both[0:MODES, cols(n)] + both[MODES : 2 * MODES, cols(n)] for n in range(len(group))
        ]

    first_stack()
    copies = exchange(0)
    for n in (7, 8, 9, 10, 5, 6, 2, 3, 11):
        loads[n].wait()
    small = cluster_ref[...] == 0
    other_operators(small)
    for f in range(FIELDS):
        base_ref[f] = sol_ref[f]
    pack_star()
    local_part()
    remote_part(0, copies)
    for group in GROUPS:
        update = lifted(group)
        for n, g in enumerate(group):
            base_ref[g] -= update[n]
    second_stack()
    copies = exchange(1)
    local_part()
    remote_part(1, copies)
    for group in GROUPS:
        update = lifted(group)
        for n, g in enumerate(group):
            out_ref[g] = base_ref[g] - update[n]


def on_device(
    n_dom,
    n_near,
    solution,
    star_matrices,
    flux_plus,
    flux_minus,
    stiffness,
    face_lift,
    face_project,
    cluster,
    neighbour_part,
    neighbour_slot,
    neighbour_face,
    orientation,
    halo_send,
):
    operands = (
        jnp.transpose(solution, (1, 0, 2)),
        jnp.transpose(star_matrices, (1, 2, 0, 3)),
        jnp.transpose(flux_plus, (1, 2, 0, 3)),
        jnp.transpose(flux_minus, (1, 2, 0, 3)),
        stiffness,
        jnp.transpose(face_lift, (2, 0, 1)),
        jnp.transpose(face_project, (1, 0, 2)),
        cluster.reshape(1, E),
        neighbour_part,
        neighbour_slot,
        neighbour_face,
        orientation,
        halo_send,
    )
    field_block = pltpu.VMEM((FIELDS, MODES, E), F32)
    step = pl.pallas_call(
        functools.partial(kernel, n_dom, n_near),
        out_shape=pltpu.VMEM((FIELDS, MODES, E), F32),
        in_specs=[pl.BlockSpec(memory_space=pltpu.HBM)] * 13,
        out_specs=pl.BlockSpec(memory_space=pltpu.VMEM),
        scratch_shapes=[pltpu.VMEM(value.shape, value.dtype) for value in operands]
        + [
            pltpu.VMEM((2, FACES + 3 * MODES, COLS), F32),
            field_block,
            field_block,
            field_block,
            pltpu.VMEM((FACES, COLS), F32),
            pltpu.VMEM((FIELDS * FACE_PAD, 4 * E), F32),
            pltpu.VMEM((3 * MODES, 3 * KPAD), BF),
            pltpu.VMEM((FACES + 3 * MODES, 3 * KPAD), BF),
            pltpu.VMEM((FACES, 3 * KPAD), BF),
            pltpu.VMEM((2 * MODES, 2 * FACES), BF),
            pltpu.VMEM((4 * E, 4 * E), BF),
            pltpu.VMEM((16 * HALO, 4 * E), BF),
            pltpu.VMEM((2 * E, 4 * E), BF),
            pltpu.VMEM((2, 4, KPAD, E), F32),
            pltpu.VMEM((2, 4, KPAD, E), F32),
            pltpu.SemaphoreType.DMA((2, 4)),
            pltpu.SemaphoreType.DMA((2, 4)),
            pltpu.SemaphoreType.DMA((13,)),
            pltpu.VMEM((FIELDS, FIELDS, 3, 8, E), F32),
            pltpu.VMEM((len(PAIRS), FIELDS, 3, 8, E), F32),
            pltpu.VMEM((2 * E, E), BF),
            pltpu.VMEM((2 * E, 2 * E), BF),
            pltpu.VMEM((len(PAIRS), MODES, E), F32),
            pltpu.VMEM((4 * E, E), BF),
            pltpu.VMEM((2, 8, E), F32),
            pltpu.VMEM((FIELDS, FIELDS, 8, E), F32),
        ],
        compiler_params=pltpu.CompilerParams(
            collective_id=0, has_side_effects=True, vmem_limit_bytes=60 * 2**20
        ),
        name="cluster_step",
    )
    out = step(*operands)
    return jnp.transpose(out, (1, 0, 2))


def solution(mesh):
    both = ("dom", "near")
    in_specs = (
        P(None, None, both),
        P(None, None, None, both),
        P(None, None, None, both),
        P(None, None, None, both),
        P(),
        P(),
        P(),
        P(both),
        P(None, both),
        P(None, both),
        P(None, both),
        P(None, both),
        P(None, both),
    )
    return jax.shard_map(
        functools.partial(on_device, mesh.shape["dom"], mesh.shape["near"]),
        mesh=mesh,
        in_specs=in_specs,
        out_specs=P(None, None, both),
        check_vma=False,
    )
```

```python
import functools
import math

import jax
import jax.numpy as jnp
from jax import lax
from jax.experimental import pallas as pl
from jax.experimental.pallas import tpu as pltpu
from jax.sharding import PartitionSpec as P

MESH = pl.DeviceIdType.MESH
MODES = 56
FIELDS = 9
FACE_MODES = 21
ORDER = 6
E = 128
HALO = 16
PACK = 64
PAIRS = ((0, 1), (2, 3), (4, 5), (6, 7), (8,))
PAIR_GROUPS = ((0, 1), (2, 3), (4,))
KPAD = 64
FACE_PAD = 24
FACES = 4 * FACE_PAD
COLS = FIELDS * E
GROUPS = ((0, 1), (2, 3), (4, 5), (6, 7), (8,))
BF = jnp.bfloat16
F32 = jnp.float32


def orbit_nodes():
    degree = ORDER - 1
    nodes = [(a, b, degree - a - b) for a in range(degree + 1) for b in range(degree + 1 - a)]
    number = {node: n for n, node in enumerate(nodes)}
    seen, orbits = set(), []
    for node in nodes:
        if node in seen:
            continue
        a, b, c = node
        orbit = [(a, b, c), (b, c, a), (c, a, b)]
        seen.update(orbit)
        orbits.append([number[member] for member in orbit])
    order = [-1] * FACE_PAD
    for o, orbit in enumerate(orbits):
        for c in range(3):
            order[c * 8 + o] = orbit[c]
    return order


ORDERED = orbit_nodes()


def weights(begin, end):
    return [
        (end ** (k + 1) - begin ** (k + 1)) / math.factorial(k + 1) for k in range(ORDER)
    ]


def dot(a, b):
    return jnp.dot(a, b, preferred_element_type=F32)


def iota(shape, dim):
    return lax.broadcasted_iota(jnp.int32, shape, dim)


def ones_where(condition):
    return jnp.where(condition, 1.0, 0.0).astype(F32)


def high_low(x):
    high = x.astype(BF).astype(F32)
    return high, x - high


def place(x, marks):
    high, rest = high_low(x)
    middle, low = high_low(rest)
    marks = marks.astype(BF)
    return dot(high.astype(BF), marks) + dot(middle.astype(BF), marks) + dot(low.astype(BF), marks)


def place_left(marks, x):
    high, rest = high_low(x)
    middle, low = high_low(rest)
    marks = marks.astype(BF)
    return dot(marks, high.astype(BF)) + dot(marks, middle.astype(BF)) + dot(marks, low.astype(BF))


def threefold(matrix):
    high, low = high_low(matrix)
    row, col = iota((MODES, 3 * KPAD), 0), iota((MODES, 3 * KPAD), 1)
    twice = ones_where((col == row) | (col == row + KPAD)).astype(BF)
    last = ones_where(col == row + 2 * KPAD).astype(BF)
    return (dot(high.astype(BF), twice) + dot(low.astype(BF), last)).astype(BF)


def kernel(
    n_dom,
    n_near,
    *refs,
):
    sources, out_ref, held = refs[:13], refs[13], refs[14:27]
    (
        sol_ref,
        star_ref,
        plus_ref,
        minus_ref,
        stiff_ref,
        lift_ref,
        proj_ref,
        cluster_ref,
        part_ref,
        slot_ref,
        nface_ref,
        turn_ref,
        halo_ref,
    ) = held
    (
        y_ref,
        first_ref,
        second_ref,
        base_ref,
        x_ref,
        g_ref,
        a_ref,
        b_ref,
        p_ref,
        l_ref,
        ohl_ref,
        ohr_ref,
        ohs_ref,
        send_buf,
        recv_buf,
        send_sem,
        recv_sem,
        load_sem,
        star8_ref,
        packed_star_ref,
        compact_ref,
        widen_ref,
        j_ref,
        pick_ref,
        slot_ints,
        minus8_ref,
    ) = refs[27:]
    loads = [
        pltpu.make_async_copy(source, target, load_sem.at[n])
        for n, (source, target) in enumerate(zip(sources, held))
    ]
    for n in (4, 0, 1, 12, 7, 8, 9, 10, 5, 6, 2, 3, 11):
        loads[n].start()
    dom, near = lax.axis_index("dom"), lax.axis_index("near")
    targets = (
        (dom, lax.rem(near + 1, n_near)),
        (dom, lax.rem(near + n_near - 1, n_near)),
        (lax.rem(dom + 1, n_dom), near),
        (lax.rem(dom + n_dom - 1, n_dom), near),
    )
    barrier = pltpu.get_barrier_semaphore()
    for target in targets:
        pl.semaphore_signal(barrier, inc=1, device_id=target, device_id_type=MESH)

    def cols(f, count=1):
        return slice(f * E, (f + count) * E)

    loads[4].wait()
    stiff = jnp.concatenate([stiff_ref[d] for d in range(3)], axis=0)
    a_ref[...] = threefold(stiff)

    held_parts = {}

    def split_into(t, f):
        high, low = high_low(t)
        zero = jnp.zeros((KPAD - MODES, E), F32)
        high = jnp.concatenate([high, zero], axis=0).astype(BF)
        low = jnp.concatenate([low, zero], axis=0).astype(BF)
        held_parts[f] = jnp.concatenate([high, low, high], axis=0)

    def multiply(matrix, rows, group, slot):
        columns = jnp.concatenate([held_parts[f] for f in group], axis=1)
        y_ref[slot, 0:rows, cols(group[0], len(group))] = dot(matrix[...], columns)

    def spread_mul(tile, y):
        return (tile[None] * y.reshape(MODES // 8, 8, E)).reshape(MODES, E)

    def star(group, slot, row0=0):
        totals = [None] * len(group)
        for d in range(3):
            for f in range(FIELDS):
                y = y_ref[slot, row0 + d * MODES : row0 + (d + 1) * MODES, cols(f)]
                for n, g in enumerate(group):
                    term = spread_mul(star8_ref[f, g, d], y)
                    totals[n] = term if totals[n] is None else totals[n] + term
        return totals

    half, rest = weights(0.0, 0.5), weights(0.5, 1.0)

    loads[0].wait()
    for group in GROUPS:
        for f in group:
            u = sol_ref[f]
            split_into(u, f)
            first_ref[f] = half[0] * u
            second_ref[f] = rest[0] * u
        multiply(a_ref, 3 * MODES, group, 0)

    for n in (1, 12):
        loads[n].wait()
    for f in range(FIELDS):
        for g in range(FIELDS):
            for d in range(3):
                star8_ref[f, g, d] = jnp.broadcast_to(star_ref[f, g, d : d + 1, :], (8, E))
    spread = ones_where(iota((HALO, E), 0) == lax.rem(iota((HALO, E), 1), HALO)).astype(BF)
    sent = dot(halo_ref[...].astype(F32).astype(BF), spread)
    for r in range(4):
        ohs_ref[:, cols(r)] = ones_where(
            sent[r : r + 1, :] == iota((2 * E, E), 0).astype(F32)
        ).astype(BF) + ones_where(
            sent[r : r + 1, :] + float(E) == iota((2 * E, E), 0).astype(F32)
        ).astype(BF)

    lane = iota((1, E), 1)
    lane_group = lane // HALO

    def first_stack():
        for k in range(ORDER - 2):
            for group in GROUPS:
                for g, t in zip(group, star(group, k % 2)):
                    split_into(t, g)
                    first_ref[g] += half[k + 1] * t
                    second_ref[g] += rest[k + 1] * t
                multiply(a_ref, 3 * MODES, group, (k + 1) % 2)
        for group in GROUPS:
            for g, t in zip(group, star(group, 0)):
                first_ref[g] += half[5] * t
                second_ref[g] += rest[5] * t

    def other_operators(small):
        backward = jnp.concatenate([stiff_ref[d].T for d in range(3)], axis=0)
        node, entry = iota((FACE_PAD, FACE_MODES), 1), iota((FACE_PAD, FACE_MODES), 0)
        chosen = entry < 0
        for spot, number in enumerate(ORDERED):
            if number >= 0:
                chosen = chosen | ((entry == spot) & (node == number))
        chosen = ones_where(chosen)
        project = jnp.concatenate([place_left(chosen, proj_ref[:, j, :]) for j in range(4)], axis=0)
        lifts = jnp.concatenate([place_left(chosen, lift_ref[:, j, :]) for j in range(4)], axis=0)
        b_ref[...] = threefold(jnp.concatenate([project, backward], axis=0))
        p_ref[...] = threefold(project)
        lift_high, lift_low = high_low(lifts.T)
        row, col = iota((FACES, 2 * FACES), 0), iota((FACES, 2 * FACES), 1)
        twice = ones_where((col == row) | (col == row + FACES)).astype(BF)
        once = ones_where(col == row).astype(BF)
        l_ref[...] = jnp.concatenate(
            [dot(lift_high.astype(BF), twice), dot(lift_low.astype(BF), once)], axis=0
        ).astype(BF)

        part, slot_of = part_ref[...], slot_ref[...]
        face_of = nface_ref[...]
        local_key = jnp.where(part == 0, face_of * E + slot_of, -1)
        slot_key = jnp.where(part > 0, (part - 1) * HALO + slot_of, -1).astype(F32)
        diagonal = iota((E, E), 0) == iota((E, E), 1)
        slot_lane = lax.rem(iota((E, E), 1), PACK).astype(F32)
        for i in range(4):
            ohl_ref[:, cols(i)] = ones_where(local_key[i : i + 1, :] == iota((4 * E, E), 0)).astype(BF)
            key = slot_key[i : i + 1, :]
            scatter = ones_where(key == iota((E, E), 0).astype(F32)).astype(BF)
            ohr_ref[0:E, cols(i)] = scatter
            ohr_ref[E : 2 * E, cols(i)] = scatter
            key_col = jnp.sum(jnp.where(diagonal, key, 0.0), axis=1, keepdims=True)
            pick_ref[i * E : (i + 1) * E, :] = ones_where(key_col == slot_lane).astype(BF)
        for n, table in enumerate((face_of, turn_ref[...])):
            line = jnp.concatenate([table[i : i + 1, :] for i in range(4)], axis=1).astype(F32)
            slot_ints[n] = dot(jnp.broadcast_to(line, (8, 4 * E)).astype(BF), pick_ref[...])
        for f in range(FIELDS):
            line = jnp.concatenate(
                [
                    jnp.concatenate(
                        [
                            jnp.broadcast_to(minus_ref[f, g, i : i + 1, :], (8, E))
                            for g in range(FIELDS)
                        ],
                        axis=0,
                    )
                    for i in range(4)
                ],
                axis=1,
            )
            high, low = high_low(line)
            both = dot(high.astype(BF), pick_ref[...]) + dot(low.astype(BF), pick_ref[...])
            minus8_ref[f] = both.reshape(FIELDS, 8, E)
        before = ones_where(iota((E, E), 0) < iota((E, E), 1)).astype(BF)
        small_row = ones_where(small)
        rank_row = dot(jnp.broadcast_to(small_row, (8, E)).astype(BF), before)[0:1]
        rank_row = jnp.where(small, rank_row, -1.0)
        square = iota((E, E), 0) == iota((E, E), 1)
        rank_col = jnp.sum(jnp.where(square, rank_row, 0.0), axis=1, keepdims=True)
        place_of = lax.rem(iota((E, E), 1), PACK).astype(F32)
        compact = ones_where(rank_col == place_of).astype(BF)
        compact_ref[0:E] = compact
        compact_ref[E : 2 * E] = compact
        source = iota((E, E), 0)
        for h in range(2):
            wide = ones_where(rank_row == (source - h * PACK).astype(F32)).astype(BF)
            widen_ref[0:E, cols(h)] = wide
            widen_ref[E : 2 * E, cols(h)] = wide

    lower = lane < PACK

    def sides(block):
        high, low = high_low(block)
        return jnp.concatenate([high.astype(BF), low.astype(BF)], axis=1)

    def pack_star():
        rows = FIELDS * 3 * 8
        for p, pair in enumerate(PAIRS):
            taken = [
                dot(sides(star8_ref[f].reshape(rows, E)), compact_ref[...]) for f in pair
            ]
            both = jnp.where(lower, taken[0], taken[1] if len(pair) == 2 else 0.0)
            packed_star_ref[p] = both.reshape(FIELDS, 3, 8, E)

    def packed_star(pairs, slot):
        fields = [g for p in pairs for g in PAIRS[p]]
        totals = dict.fromkeys(fields)
        for d in range(3):
            for q in range(len(PAIRS)):
                y = y_ref[slot, d * MODES : (d + 1) * MODES, cols(q)]
                for g in fields:
                    term = spread_mul(packed_star_ref[q, g, d], y)
                    totals[g] = term if totals[g] is None else totals[g] + term
        folded = []
        for p in pairs:
            one = totals[PAIRS[p][0]]
            if len(PAIRS[p]) == 2:
                two = totals[PAIRS[p][1]]
                folded.append(
                    jnp.where(lower, one, two) + pltpu.roll(jnp.where(lower, two, one), PACK, 1)
                )
            else:
                folded.append(jnp.where(lower, one + pltpu.roll(one, PACK, 1), 0.0))
        return folded

    def second_stack():
        for group in PAIR_GROUPS:
            for p in group:
                taken = dot(
                    sides(jnp.concatenate([base_ref[f] for f in PAIRS[p]], axis=0)),
                    compact_ref[...],
                )
                taken = [taken[n * MODES : (n + 1) * MODES] for n in range(len(PAIRS[p]))]
                u = jnp.where(lower, taken[0], taken[1] if len(taken) == 2 else 0.0)
                split_into(u, p)
                j_ref[p] = half[0] * u
            multiply(a_ref, 3 * MODES, group, 0)
        for k in range(ORDER - 2):
            for group in PAIR_GROUPS:
                for p, t in zip(group, packed_star(group, k % 2)):
                    split_into(t, p)
                    j_ref[p] += half[k + 1] * t
                multiply(a_ref, 3 * MODES, group, (k + 1) % 2)
        for group in PAIR_GROUPS:
            for p, t in zip(group, packed_star(group, 0)):
                wide = dot(sides(j_ref[p] + half[5] * t), widen_ref[...])
                for n, f in enumerate(PAIRS[p]):
                    first_ref[f] = jnp.where(small, wide[:, cols(n)], second_ref[f])

    def exchange(phase):
        copies = []
        highs, lows = [], []
        for f in range(FIELDS):
            high, low = high_low(first_ref[f])
            highs.append(high)
            lows.append(low)
        stacked = jnp.concatenate(
            [
                jnp.concatenate(highs, axis=0).astype(BF),
                jnp.concatenate(lows, axis=0).astype(BF),
            ],
            axis=1,
        )
        for pair in ((0, 1), (2, 3)):
            taken = dot(stacked, ohs_ref[:, cols(pair[0], 2)])
            for n, r in enumerate(pair):
                block = taken[:, cols(n)]
                packed = block[0:MODES]
                for f in range(1, 8):
                    packed = jnp.where(lane_group == f, block[f * MODES : (f + 1) * MODES], packed)
                tail = block[8 * MODES : 8 * MODES + 8]
                for k in range(1, 7):
                    start = 8 * MODES + 8 * k
                    tail = jnp.where(lane_group == k, block[start : start + 8], tail)
                send_buf[phase, r] = jnp.concatenate([packed, tail], axis=0)
            if phase == 0 and pair[0] == 0:
                pl.semaphore_wait(barrier, 4)
            for r in pair:
                copy = pltpu.make_async_remote_copy(
                    src_ref=send_buf.at[phase, r],
                    dst_ref=recv_buf.at[phase, r],
                    send_sem=send_sem.at[phase, r],
                    recv_sem=recv_sem.at[phase, r],
                    device_id=targets[r],
                    device_id_type=MESH,
                )
                copy.start()
                copies.append(copy)
        return copies

    def gather(blocks, marks):
        tall = []
        for block in blocks:
            high, low = high_low(block)
            tall.append(jnp.concatenate([high, low], axis=0).astype(BF))
        both = dot(jnp.concatenate(tall, axis=1), marks[...])
        rows = FIELDS * FACE_PAD
        return both[0:rows] + both[rows : 2 * rows]

    def by_field(read):
        return jnp.concatenate([read(f) for f in range(FIELDS)], axis=0)

    def rotated(raw, for_one, for_two):
        v = [raw[c * 8 : (c + 1) * 8] for c in range(3)]
        return jnp.concatenate(
            [
                jnp.where(for_one, v[(c + 1) % 3], jnp.where(for_two, v[(c + 2) % 3], v[c]))
                for c in range(3)
            ],
            axis=0,
        )

    def local_part():
        for group in GROUPS:
            for f in group:
                split_into(first_ref[f], f)
            multiply(b_ref, FACES + 3 * MODES, group, 0)
        g_ref[...] = gather(
            [
                by_field(lambda f: y_ref[0, j * FACE_PAD : (j + 1) * FACE_PAD, cols(f)])
                for j in range(4)
            ],
            ohl_ref,
        )
        for i in range(4):
            totals = [None] * FIELDS
            turn = turn_ref[i : i + 1, :]
            for f in range(FIELDS):
                y = y_ref[0, i * FACE_PAD : (i + 1) * FACE_PAD, cols(f)]
                z = rotated(g_ref[f * FACE_PAD : (f + 1) * FACE_PAD, cols(i)], turn == 1, turn == 2)
                for g in range(FIELDS):
                    term = plus_ref[f, g, i : i + 1, :] * y + minus_ref[f, g, i : i + 1, :] * z
                    totals[g] = term if totals[g] is None else totals[g] + term
            for g in range(FIELDS):
                x_ref[i * FACE_PAD : (i + 1) * FACE_PAD, cols(g)] = totals[g]
        for group in GROUPS:
            for g, v in zip(group, star(group, 0, FACES)):
                base_ref[g] += v

    def remote_part(phase, copies):
        for copy in copies:
            copy.wait()
        rolled = []
        for r in range(4):
            block = recv_buf[phase, r]
            rolled.append(
                [block if c == 0 else pltpu.roll(block, c * HALO, 1) for c in range(8)]
            )

        def collect(at, rows):
            value = None
            for spot in range(8):
                r = spot % 4
                piece = rolled[r][(spot - at) % 8][rows]
                value = piece if value is None else jnp.where(lane_group == spot, piece, value)
            return value

        for group in GROUPS:
            for f in group:
                if f < 8:
                    split_into(collect(f, slice(0, MODES)), f)
                else:
                    tiles = [collect(k, slice(MODES, MODES + 8)) for k in range(7)]
                    split_into(jnp.concatenate(tiles, axis=0), f)
            multiply(p_ref, FACES, group, 1)

        face, turn = slot_ints[0, 0:1, :], slot_ints[1, 0:1, :]
        totals = [None] * FIELDS
        for f in range(FIELDS):
            t = [y_ref[1, j * FACE_PAD : (j + 1) * FACE_PAD, cols(f)] for j in range(4)]
            own = jnp.where(
                face == 0.0, t[0], jnp.where(face == 1.0, t[1], jnp.where(face == 2.0, t[2], t[3]))
            )
            y = rotated(own, turn == 1.0, turn == 2.0)
            for g in range(FIELDS):
                term = (minus8_ref[f, g][None] * y.reshape(3, 8, E)).reshape(FACE_PAD, E)
                totals[g] = term if totals[g] is None else totals[g] + term
        g_ref[...] = dot(sides(jnp.concatenate(totals, axis=0)), ohr_ref[...])

    def outside(group):
        return [
            x_ref[:, cols(g)]
            + jnp.concatenate(
                [g_ref[g * FACE_PAD : (g + 1) * FACE_PAD, cols(i)] for i in range(4)], axis=0
            )
            for g in group
        ]

    def lifted(group):
        parts = []
        for g, flux in zip(group, outside(group)):
            high, low = high_low(flux)
            parts.append(jnp.concatenate([high.astype(BF), low.astype(BF)], axis=0))
        both = dot(l_ref[...], jnp.concatenate(parts, axis=1))
        return [
            both[0:MODES, cols(n)] + both[MODES : 2 * MODES, cols(n)] for n in range(len(group))
        ]

    first_stack()
    copies = exchange(0)
    for n in (7, 8, 9, 10, 5, 6, 2, 3, 11):
        loads[n].wait()
    small = cluster_ref[...] == 0
    other_operators(small)
    for f in range(FIELDS):
        base_ref[f] = sol_ref[f]
    pack_star()
    local_part()
    remote_part(0, copies)
    for group in GROUPS:
        update = lifted(group)
        for n, g in enumerate(group):
            base_ref[g] -= update[n]
    second_stack()
    copies = exchange(1)
    local_part()
    remote_part(1, copies)
    for group in GROUPS:
        update = lifted(group)
        for n, g in enumerate(group):
            out_ref[g] = base_ref[g] - update[n]


def on_device(
    n_dom,
    n_near,
    solution,
    star_matrices,
    flux_plus,
    flux_minus,
    stiffness,
    face_lift,
    face_project,
    cluster,
    neighbour_part,
    neighbour_slot,
    neighbour_face,
    orientation,
    halo_send,
):
    operands = (
        jnp.transpose(solution, (1, 0, 2)),
        jnp.transpose(star_matrices, (1, 2, 0, 3)),
        jnp.transpose(flux_plus, (1, 2, 0, 3)),
        jnp.transpose(flux_minus, (1, 2, 0, 3)),
        stiffness,
        jnp.transpose(face_lift, (2, 0, 1)),
        jnp.transpose(face_project, (1, 0, 2)),
        cluster.reshape(1, E),
        neighbour_part,
        neighbour_slot,
        neighbour_face,
        orientation,
        halo_send,
    )
    field_block = pltpu.VMEM((FIELDS, MODES, E), F32)
    step = pl.pallas_call(
        functools.partial(kernel, n_dom, n_near),
        out_shape=pltpu.VMEM((FIELDS, MODES, E), F32),
        in_specs=[pl.BlockSpec(memory_space=pltpu.HBM)] * 13,
        out_specs=pl.BlockSpec(memory_space=pltpu.VMEM),
        scratch_shapes=[pltpu.VMEM(value.shape, value.dtype) for value in operands]
        + [
            pltpu.VMEM((2, FACES + 3 * MODES, COLS), F32),
            field_block,
            field_block,
            field_block,
            pltpu.VMEM((FACES, COLS), F32),
            pltpu.VMEM((FIELDS * FACE_PAD, 4 * E), F32),
            pltpu.VMEM((3 * MODES, 3 * KPAD), BF),
            pltpu.VMEM((FACES + 3 * MODES, 3 * KPAD), BF),
            pltpu.VMEM((FACES, 3 * KPAD), BF),
            pltpu.VMEM((2 * MODES, 2 * FACES), BF),
            pltpu.VMEM((4 * E, 4 * E), BF),
            pltpu.VMEM((16 * HALO, 4 * E), BF),
            pltpu.VMEM((2 * E, 4 * E), BF),
            pltpu.VMEM((2, 4, KPAD, E), F32),
            pltpu.VMEM((2, 4, KPAD, E), F32),
            pltpu.SemaphoreType.DMA((2, 4)),
            pltpu.SemaphoreType.DMA((2, 4)),
            pltpu.SemaphoreType.DMA((13,)),
            pltpu.VMEM((FIELDS, FIELDS, 3, 8, E), F32),
            pltpu.VMEM((len(PAIRS), FIELDS, 3, 8, E), F32),
            pltpu.VMEM((2 * E, E), BF),
            pltpu.VMEM((2 * E, 2 * E), BF),
            pltpu.VMEM((len(PAIRS), MODES, E), F32),
            pltpu.VMEM((4 * E, E), BF),
            pltpu.VMEM((2, 8, E), F32),
            pltpu.VMEM((FIELDS, FIELDS, 8, E), F32),
        ],
        compiler_params=pltpu.CompilerParams(
            collective_id=0, has_side_effects=True, vmem_limit_bytes=60 * 2**20
        ),
        name="cluster_step",
    )
    out = step(*operands)
    return jnp.transpose(out, (1, 0, 2))


def solution(mesh):
    both = ("dom", "near")
    in_specs = (
        P(None, None, both),
        P(None, None, None, both),
        P(None, None, None, both),
        P(None, None, None, both),
        P(),
        P(),
        P(),
        P(both),
        P(None, both),
        P(None, both),
        P(None, both),
        P(None, both),
        P(None, both),
    )
    return jax.shard_map(
        functools.partial(on_device, mesh.shape["dom"], mesh.shape["near"]),
        mesh=mesh,
        in_specs=in_specs,
        out_specs=P(None, None, both),
        check_vma=False,
    )
```
